32 devices in a mesh: dp: 16 (over z, y, x), mp: 2 (over core).
Axes of the slice: x: 2, y: 2, z: 4, core: 2. Of those that a mesh axis runs over, the one named last changes fastest.
Arguments:
- features: bfloat16 [4096, 768], P('dp', 'mp'), may hold values from -0.21875 to 0.21875
- labels: int32 [4096], P('dp'), may hold values from 0 to 16383, as said below
- queries: bfloat16 [4096, 768], P('dp', 'mp'), may hold values from -240 to 240
- bank: float32 [16384, 768], P('dp', 'mp'), may hold values from -0.21875 to 0.21875
- old_conc: float32 [16384], P('dp'), may hold values from 0.4 to 0.6
- neg_index: int32 [1024], replicated, may hold values from 0 to 16383, as said below
Outputs:
- new_bank: float32 [16384, 768], P('dp', 'mp')
- new_conc: float32 [16384], P('dp')
- loss: float32 [4096], P('dp')
- grad: float32 [4096, 768], P('dp', 'mp')
The draws below stay inside these ranges and needn't reach their ends.
Inputs may be any that keep to these rules, and one draw needn't show every extreme that they name: In each aligned block of 256 rows, at most 48 labels fall in any one range of 1024 consecutive prototypes starting at a multiple of 1024; one such range receives exactly 48 labels from every block. `neg_index`: entries j * 64 to (j + 1) * 64 - 1 are distinct prototypes of the range j * 1024 to (j + 1) * 1024 - 1.
All inputs are finite; a program needn't handle non-finite values.
Results may differ from the reference program's by a relative error of at most 0.0074.
Values may be sent and summed in bfloat16 or wider, within the bound.
No kernel may reach another device: no remote copies, remote signals or barrier semaphores. Data moves between devices by JAX's collectives and lax.ppermute only.
A program may use at most 64 MiB of HBM per device.

```python
import math
import jax
import jax.numpy as jnp
from jax import lax

D = 768
PROTO_DEV = 1024
FEAT_DEV = 256
NEG_DEV = 64
CAP = 48
PROTOS = 16384
FEATS = 4096
N_DP = 16


def draw_labels(key, part):
    slot_total = N_DP * CAP
    slot_owner = jnp.arange(slot_total, dtype=jnp.int32) // CAP
    hottest = jax.random.randint(jax.random.fold_in(key, 7), (), 0, N_DP)
    heavy = jax.random.permutation(jax.random.fold_in(key, 8), N_DP) < max(N_DP // 8, 1)
    factor = jnp.where(heavy[slot_owner], 4, 1)

    def one_block(block_key):
        key_score, key_order, key_local = jax.random.split(block_key, 3)
        score = jax.random.randint(key_score, (slot_total,), 0, 2 ** 16) * factor
        score = score * slot_total + jnp.arange(slot_total, dtype=jnp.int32)
        score = jnp.where(slot_owner == hottest, -1, score)
        chosen = lax.top_k(score, FEAT_DEV - CAP)[1]
        owners = jnp.concatenate([jnp.full((CAP,), hottest, jnp.int32), slot_owner[chosen]])
        owners = jax.random.permutation(key_order, owners)
        local = jax.random.randint(key_local, (FEAT_DEV,), 0, PROTO_DEV)
        return owners * PROTO_DEV + local
    keys = jax.random.split(jax.random.fold_in(key, 9), N_DP)
    return jax.vmap(one_block)(keys).reshape(-1).astype(jnp.int32)


def draw_neg_index(key, part):
    score = jax.random.randint(jax.random.fold_in(key, 11), (N_DP, PROTO_DEV), 0, 2 ** 16)
    score = score * PROTO_DEV + jnp.arange(PROTO_DEV, dtype=jnp.int32)[None, :]
    local = lax.top_k(score, NEG_DEV)[1]
    owners = jnp.arange(N_DP, dtype=jnp.int32)[:, None]
    return (owners * PROTO_DEV + local).reshape(-1).astype(jnp.int32)


def draw_queries(key, part):
    rows_all = FEAT_DEV * N_DP
    key_base = jax.random.fold_in(key, 21)
    key_rows = jax.random.fold_in(key, 22)
    base = jnp.clip(jax.random.normal(key_base, (rows_all, D), jnp.float32), -6.0, 6.0)
    boosted = jax.random.randint(key_rows, (rows_all,), 0, 32) == 0
    scale = jnp.where(boosted, 40.0, 1.0)
    return (base * scale[:, None]).astype(jnp.bfloat16)


def levels(rng, dims, shards, low, high):
    def one(position, blocks):
        heights = jax.random.uniform(jax.random.fold_in(jax.random.fold_in(rng, 6), position), (blocks,), jnp.float32, low / len(shards), high / len(shards))
        return jnp.repeat(jnp.exp(heights), dims[position] // blocks).reshape((-1,) + (1,) * (len(dims) - position - 1))

    level = one(*shards[0])
    for cut in shards[1:]:
        level = level * one(*cut)
    return level


def centred(own_key, dims, spread, limit, pieces=(), held_as=jnp.bfloat16):
    drawn = spread * jax.random.normal(own_key, dims, jnp.float32)
    if pieces:
        drawn = drawn * levels(own_key, dims, pieces, -0.22, 0.18)
    return jnp.clip(drawn, -limit, limit).astype(held_as)


def setup_inputs(seed: int = 0) -> dict:
    arg_keys = jax.random.split(jax.random.key(seed), 7)
    return {
        "features": centred(arg_keys[0], (FEATS, D), D ** -0.5, 0.21875, ((0, 16), (1, 2))),
        "labels": draw_labels(jax.random.fold_in(arg_keys[6], 71), 0),
        "queries": draw_queries(jax.random.fold_in(arg_keys[6], 71), 0),
        "bank": centred(arg_keys[3], (PROTOS, D), D ** -0.5, 0.21875, ((0, 16), (1, 2)), jnp.float32),
        "old_conc": jnp.clip(0.4 + 0.20000002 * jax.random.uniform(arg_keys[4], (PROTOS,), jnp.float32) ** levels(arg_keys[4], (PROTOS,), ((0, 16),), -0.2, 0.2), 0.4, 0.6),
        "neg_index": draw_neg_index(jax.random.fold_in(arg_keys[6], 71), 0),
    }


def reference(features, labels, queries, bank, old_conc, neg_index):
    protos = bank.shape[0]
    feat32 = features.astype(jnp.float32)
    sums = jax.ops.segment_sum(feat32, labels, num_segments=protos)
    counts = jax.ops.segment_sum(jnp.ones(labels.shape, jnp.float32), labels, num_segments=protos)
    touched = counts > 0
    safe_counts = jnp.maximum(counts, 1.0)
    blended = 0.5 * bank + 0.5 * sums / safe_counts[:, None]
    new_bank = jnp.where(touched[:, None], blended, bank)
    differ = feat32 - new_bank[labels]
    dist = jnp.sqrt(lax.optimization_barrier(jnp.sum(differ * differ, axis=1)) + 0.25)
    dist_sums = jax.ops.segment_sum(dist, labels, num_segments=protos)
    new_conc = jnp.where(touched, dist_sums / (safe_counts * jnp.log(safe_counts + 10.0)), old_conc)
    scaled = (new_bank / new_conc[:, None]).astype(jnp.bfloat16)
    negs = scaled[neg_index]
    posrows = scaled[labels]
    positive = lax.optimization_barrier(jnp.sum(queries.astype(jnp.float32) * posrows.astype(jnp.float32), axis=1))
    rows_all = queries.shape[0]
    block = math.gcd(rows_all, 1024)
    blocks = rows_all // block

    def one_block(args):
        query_block, pos_block, prow_block = args
        negative = jnp.dot(query_block, negs.T, preferred_element_type=jnp.float32)
        top = jnp.maximum(lax.optimization_barrier(jnp.max(negative, axis=1)), pos_block)
        expneg = jnp.exp(negative - top[:, None])
        exppos = jnp.exp(pos_block - top)
        total = lax.optimization_barrier(jnp.sum(expneg, axis=1)) + exppos
        loss_block = jnp.log(total) + top - pos_block
        weight = (expneg / total[:, None]).astype(jnp.bfloat16)
        grad_block = jnp.dot(weight, negs, preferred_element_type=jnp.float32)
        grad_block = grad_block + (exppos / total - 1.0)[:, None] * prow_block.astype(jnp.float32)
        return (loss_block, grad_block)
    loss, grad = lax.map(one_block, (queries.reshape(blocks, block, -1), positive.reshape(blocks, block), posrows.reshape(blocks, block, -1)))
    return (new_bank, new_conc, loss.reshape(rows_all), grad.reshape(rows_all, -1))
```

```python
import functools

import jax
import jax.numpy as jnp
from jax import lax
from jax.experimental import pallas as pl
from jax.experimental.pallas import tpu as pltpu
from jax.sharding import PartitionSpec as P

F32 = jnp.float32
BF16 = jnp.bfloat16
I32 = jnp.int32
LANES = 128


def call(kernel, outs, *args, flops=0, in_smem=()):
    moved = sum(a.size * a.dtype.itemsize for a in args) + sum(o.size * o.dtype.itemsize for o in outs)
    specs = [
        pl.BlockSpec(memory_space=pltpu.SMEM if k in in_smem else pltpu.VMEM) for k in range(len(args))
    ]
    return pl.pallas_call(
        kernel,
        out_shape=list(outs),
        in_specs=specs,
        out_specs=[pl.BlockSpec(memory_space=pltpu.VMEM) for _ in outs],
        compiler_params=pltpu.CompilerParams(vmem_limit_bytes=40 * 2**20),
        cost_estimate=pl.CostEstimate(flops=flops, bytes_accessed=moved, transcendentals=0),
    )(*args)


def shape(dims, dtype):
    return jax.ShapeDtypeStruct(dims, dtype)


def nt(a, b):
    return lax.dot_general(a, b, (((1,), (1,)), ((), ())), preferred_element_type=F32)


def nn(a, b):
    return jnp.dot(a, b, preferred_element_type=F32)


def to_col(row):
    return jnp.transpose(jnp.broadcast_to(row, (LANES, row.shape[1])))


def to_row(col):
    return jnp.transpose(jnp.broadcast_to(col, (col.shape[0], LANES)))[0:1, :]


def upper(rows):
    before = lax.broadcasted_iota(I32, (rows, rows), 0)
    return jnp.where(before <= lax.broadcasted_iota(I32, (rows, rows), 1), 1.0, 0.0).astype(BF16)


def pack_kernel(owners, owned, capacity, label_ref, feat_ref, send_ref, slot_ref):
    rows = label_ref.shape[1]
    label = label_ref[...]
    start = lax.broadcasted_iota(I32, (owners, rows), 0) * owned
    mine = (label >= start) & (label < start + owned)
    table = jnp.where(mine, 1.0, 0.0)
    running = nn(table.astype(BF16), upper(rows))
    place = running - 1.0 + (lax.broadcasted_iota(I32, (owners, rows), 0) * capacity).astype(F32)
    slot = jnp.sum(jnp.where(mine, place, 0.0), axis=0, keepdims=True).astype(I32)
    slot_ref[...] = slot
    pick = jnp.where(lax.broadcasted_iota(I32, (owners * capacity, rows), 0) == slot, 1.0, 0.0).astype(BF16)
    send_ref[...] = nn(pick, feat_ref[...]).astype(BF16)


def ids_kernel(owned, capacity, self_ref, label_ref, row_ref, col_ref):
    owners, rows = label_ref.shape
    slots = row_ref.shape[1]
    me = self_ref[0]
    local = label_ref[...] - me * owned
    mine = (local >= 0) & (local < owned)
    rank = nn(jnp.where(mine, 1.0, 0.0).astype(BF16), upper(rows)) - 1.0
    rank = jnp.where(mine, rank, -1.0)
    value = local.astype(F32) + 1.0
    lane = lax.broadcasted_iota(I32, (owners, LANES), 1)
    table = jnp.zeros((owners, LANES), F32)
    for j in range(capacity):
        found = jnp.sum(jnp.where(rank == float(j), value, 0.0), axis=1, keepdims=True)
        table = jnp.where(lane == j, found, table)
    high = jnp.floor(table * (1.0 / 32.0))
    low = table - 32.0 * high
    place = lax.broadcasted_iota(I32, (LANES, slots), 1).astype(F32)
    within = place - capacity * jnp.floor((place + 0.5) * (1.0 / capacity))
    spread = jnp.where(within == lax.broadcasted_iota(I32, (LANES, slots), 0).astype(F32), 1.0, 0.0).astype(BF16)
    wide = 32.0 * nn(high.astype(BF16), spread) + nn(low.astype(BF16), spread)
    first = (lax.broadcasted_iota(I32, (owners, slots), 0) ^ me) * capacity
    spot = lax.broadcasted_iota(I32, (owners, slots), 1)
    own_block = (spot >= first) & (spot < first + capacity)
    ids = jnp.sum(jnp.where(own_block, wide, 0.0), axis=0, keepdims=True)
    ids = jnp.where(ids > 0.5, ids - 1.0, float(owned))
    row_ref[...] = ids.astype(I32)
    col_ref[...] = to_col(ids).astype(I32)


def blend(bank, sums, counts):
    safe = jnp.maximum(counts, 1.0)
    return jnp.where(counts > 0, 0.5 * bank + 0.5 * sums / safe, bank)


def mean_kernel(row_ref, col_ref, neg_ref, got_ref, bank_ref, new_ref, pack_ref):
    slots, width = got_ref.shape
    negs = neg_ref.shape[0]
    half = negs // 2
    ids = row_ref[...]
    got = got_ref[...]
    same = jnp.where(col_ref[:, 0:1] == ids, 1.0, 0.0)
    new = blend(bank_ref[0:slots, :], nn(same.astype(BF16), got), jnp.sum(same, axis=1, keepdims=True))
    new_ref[0:slots, :] = new
    differ = got.astype(F32) - new
    squared = to_row(jnp.sum(differ * differ, axis=1, keepdims=True))
    same = jnp.where(neg_ref[:, 0:1] == ids, 1.0, 0.0)
    new = blend(bank_ref[slots:, :], nn(same.astype(BF16), got), jnp.sum(same, axis=1, keepdims=True))
    new_ref[slots:, :] = new[0:half]
    pack_ref[0:half, :] = new[half:]
    for k in range(slots // width):
        pack_ref[half + k : half + k + 1, :] = squared[:, k * width : (k + 1) * width]


def concentration(same, dist, old):
    counts = jnp.sum(jnp.where(same, 1.0, 0.0), axis=1, keepdims=True)
    total = jnp.sum(jnp.where(same, dist, 0.0), axis=1, keepdims=True)
    safe = jnp.maximum(counts, 1.0)
    return jnp.where(counts > 0, total / (safe * jnp.log(safe + 10.0)), old)


def scale_kernel(row_ref, col_ref, neg_ref, old_ref, new_ref, pack_ref, other_ref, slot_ref, full_ref, dist_ref):
    slots, width = slot_ref.shape
    half = full_ref.shape[0]
    ids = row_ref[...]
    tail = slice(half, half + slots // width)
    squared = pack_ref[tail, :] + other_ref[tail, :]
    squared = jnp.concatenate([squared[k : k + 1, :] for k in range(slots // width)], axis=1)
    dist = jnp.sqrt(squared + 0.25)
    dist_ref[...] = dist
    conc = concentration(col_ref[:, 0:1] == ids, dist, 1.0)
    slot_ref[...] = (new_ref[0:slots, :] / conc).astype(BF16)
    conc = concentration(neg_ref[0:half, 0:1] == ids, dist, old_ref[:, 0:1])
    full_ref[:, 0:width] = (new_ref[slots:, :] / conc).astype(BF16)
    full_ref[:, width:] = (other_ref[0:half, :] / conc).astype(BF16)


def owner_kernel(row_ref, col_ref, dist_ref, got_ref, bank_ref, old_ref, new_ref, conc_ref):
    block = bank_ref.shape[0]
    slots = got_ref.shape[0]
    base = pl.program_id(0) * block
    same = jnp.where(lax.broadcasted_iota(I32, (block, slots), 0) + base == row_ref[...], 1.0, 0.0)
    sums = nn(same.astype(BF16), got_ref[...])
    new_ref[...] = blend(bank_ref[...], sums, jnp.sum(same, axis=1, keepdims=True))
    turned = lax.broadcasted_iota(I32, (slots, block), 1) + base == col_ref[:, 0:1]
    counts = jnp.sum(jnp.where(turned, 1.0, 0.0), axis=0, keepdims=True)
    total = jnp.sum(jnp.where(turned, to_col(dist_ref[...])[:, 0:1], 0.0), axis=0, keepdims=True)
    safe = jnp.maximum(counts, 1.0)
    conc_ref[...] = jnp.where(counts > 0, total / (safe * jnp.log(safe + 10.0)), old_ref[...])


def owner_call(row, col, dist, got, bank, old):
    owned, width = bank.shape
    slots = got.shape[0]
    block = 256
    whole = lambda k: (0, 0)
    return pl.pallas_call(
        owner_kernel,
        grid=(owned // block,),
        in_specs=[
            pl.BlockSpec((1, slots), whole),
            pl.BlockSpec((slots, LANES), whole),
            pl.BlockSpec((1, slots), whole),
            pl.BlockSpec((slots, width), whole),
            pl.BlockSpec((block, width), lambda k: (k, 0)),
            pl.BlockSpec((1, block), lambda k: (0, k)),
        ],
        out_specs=[pl.BlockSpec((block, width), lambda k: (k, 0)), pl.BlockSpec((1, block), lambda k: (0, k))],
        out_shape=[shape((owned, width), F32), shape((1, owned), F32)],
        compiler_params=pltpu.CompilerParams(vmem_limit_bytes=40 * 2**20),
        cost_estimate=pl.CostEstimate(
            flops=2 * owned * slots * width, bytes_accessed=8 * owned * width, transcendentals=0
        ),
    )(row, col, dist, got, bank, old)


def flash_kernel(width, mine_ref, other_ref, *refs):
    parts, (keep_ref, stats_ref, send_ref) = refs[:-3], refs[-3:]
    rows = mine_ref.shape[0]
    mine, other = mine_ref[...], other_ref[...]
    logits = [nt(mine, p[:, 0:width]) + nt(other, p[:, width:]) for p in parts]
    top = functools.reduce(jnp.maximum, [jnp.max(l, axis=1, keepdims=True) for l in logits])
    total = jnp.zeros((rows, 1), F32)
    grad = jnp.zeros((rows, 2 * width), F32)
    for l, p in zip(logits, parts):
        weight = jnp.exp(l - top)
        total = total + jnp.sum(weight, axis=1, keepdims=True)
        grad = grad + nn(weight.astype(BF16), p[...])
    keep_ref[...] = grad[:, 0:width]
    send_ref[0:rows, :] = grad[:, width:]
    stats = jnp.concatenate([to_row(top), to_row(total)], axis=0)
    stats_ref[0:2, :] = stats
    send_ref[rows : rows + 2, 0:rows] = stats


def positive_kernel(slot_ref, back_ref, query_ref, rows_ref, part_ref):
    rows, slots = query_ref.shape[0], back_ref.shape[0]
    slot = to_col(slot_ref[...].astype(F32))[:, 0:1].astype(I32)
    pick = jnp.where(lax.broadcasted_iota(I32, (rows, slots), 1) == slot, 1.0, 0.0).astype(BF16)
    found = nn(pick, back_ref[...])
    rows_ref[...] = found.astype(BF16)
    part = to_row(jnp.sum(query_ref[...].astype(F32) * found, axis=1, keepdims=True))
    part_ref[...] = jnp.broadcast_to(part, part_ref.shape)


def final_kernel(self_ref, part_ref, far_ref, stats_ref, keep_ref, sent_ref, rows_ref, loss_ref, grad_ref):
    rows = keep_ref.shape[0]
    first = self_ref[0] == 0
    here, there = stats_ref[0:2, :], sent_ref[rows : rows + 2, 0:rows]
    low = jnp.where(first, here, there)
    high = jnp.where(first, there, here)
    positive = part_ref[0:1, :] + far_ref[0:1, :]
    top = jnp.maximum(jnp.maximum(low[0:1], high[0:1]), positive)
    exppos = jnp.exp(positive - top)
    total = low[1:2] * jnp.exp(low[0:1] - top) + high[1:2] * jnp.exp(high[0:1] - top) + exppos
    loss_ref[...] = jnp.log(total) + top - positive
    mine = to_col(jnp.exp(here[0:1] - top) / total)[:, 0:1]
    other = to_col(jnp.exp(there[0:1] - top) / total)[:, 0:1]
    pull = to_col(exppos / total - 1.0)[:, 0:1]
    grad_ref[...] = keep_ref[...] * mine + sent_ref[0:rows, :] * other + pull * rows_ref[...].astype(F32)


def swap(value):
    return lax.ppermute(value, "mp", [(0, 1), (1, 0)])


def hop(value, count, bits):
    return lax.ppermute(value, "dp", [(k, k ^ bits) for k in range(count)])


def spread(value, count):
    held, done = value, 1
    pieces = [value]
    while done < count:
        step = min(4, count // done)
        stride = count // (done * step)
        pieces = [held] + [hop(held, count, stride * k) for k in range(1, step)]
        done *= step
        if done < count:
            held = jnp.concatenate(pieces, axis=0)
    return pieces


def gathered_labels(labels, count):
    held = labels.reshape(1, -1)
    bit = 1
    while bit < count:
        held = jnp.concatenate([held, hop(held, count, bit)], axis=0)
        bit *= 2
    return held


def body(features, labels, queries, bank, old_conc, neg_index):
    count = lax.axis_size("dp")
    me, core = lax.axis_index("dp"), lax.axis_index("mp")
    owned, width = bank.shape
    rows = features.shape[0]
    capacity = 3 * rows // count
    slots = count * capacity
    negs = neg_index.shape[0] // count
    half = negs // 2
    me_ref, core_ref = me.astype(I32).reshape(1), core.astype(I32).reshape(1)

    label_row = labels.reshape(1, rows)
    send, slot = call(
        functools.partial(pack_kernel, count, owned, capacity),
        (shape((slots, width), BF16), shape((1, rows), I32)),
        label_row, features, flops=2 * slots * rows * width,
    )
    got = lax.all_to_all(send.reshape(count, capacity, width), "dp", split_axis=0, concat_axis=0)
    got = got.reshape(slots, width)

    query_far = swap(queries)
    ids_row, ids_col = call(
        functools.partial(ids_kernel, owned, capacity),
        (shape((1, slots), I32), shape((slots, LANES), I32)),
        me_ref, gathered_labels(labels, count), in_smem=(0,),
    )
    start = me * negs
    near = lax.dynamic_slice_in_dim(neg_index, start + core * half, half) - me * owned
    far = lax.dynamic_slice_in_dim(neg_index, start + (1 - core) * half, half) - me * owned
    both = jnp.concatenate([near, far])
    held = bank[jnp.concatenate([jnp.minimum(ids_row.reshape(slots), owned - 1), both])]
    neg_col = jnp.broadcast_to(both[:, None], (negs, LANES))
    old_col = jnp.broadcast_to(old_conc[near][:, None], (half, LANES))

    extra = 8 * -(-(slots // width) // 8)
    new, pack = call(
        mean_kernel,
        (shape((slots + half, width), F32), shape((half + extra, width), F32)),
        ids_row, ids_col, neg_col, got, held, flops=2 * (slots + negs) * slots * width,
    )
    scaled, full, dist = call(
        scale_kernel,
        (shape((slots, width), BF16), shape((half, 2 * width), BF16), shape((1, slots), F32)),
        ids_row, ids_col, neg_col, old_col, new, pack, swap(pack),
    )
    back = lax.all_to_all(scaled.reshape(count, capacity, width), "dp", split_axis=0, concat_axis=0)
    pieces = spread(full, count)
    new_bank, new_conc = owner_call(ids_row, ids_col, dist, got, bank, old_conc.reshape(1, owned))
    keep, stats, sent = call(
        functools.partial(flash_kernel, width),
        (shape((rows, width), F32), shape((8, rows), F32), shape((rows + 8, width), F32)),
        queries, query_far, *pieces, flops=8 * rows * half * count * width,
    )
    sent = swap(sent)
    found, part = call(
        positive_kernel,
        (shape((rows, width), BF16), shape((8, rows), F32)),
        slot, back.reshape(slots, width), queries, flops=2 * slots * rows * width,
    )
    loss, grad = call(
        final_kernel,
        (shape((1, rows), F32), shape((rows, width), F32)),
        core_ref, part, swap(part), stats, keep, sent, found, in_smem=(0,),
    )
    return (new_bank, new_conc.reshape(owned), loss.reshape(rows), grad)


def solution(mesh):
    placed = (P("dp", "mp"), P("dp"), P("dp", "mp"), P("dp", "mp"), P("dp"), P())
    return jax.shard_map(
        body,
        mesh=mesh,
        in_specs=placed,
        out_specs=(P("dp", "mp"), P("dp"), P("dp"), P("dp", "mp")),
        check_vma=False,
    )
```

```python
import functools

import jax
import jax.numpy as jnp
from jax import lax
from jax.experimental import pallas as pl
from jax.experimental.pallas import tpu as pltpu
from jax.sharding import PartitionSpec as P

F32 = jnp.float32
BF16 = jnp.bfloat16
I32 = jnp.int32
LANES = 128
VMEM = 24 * 2**20


def call(kernel, outs, *args, flops=0, smem=(), hbm=(), out_hbm=(), free=(), out_free=(), scratch=()):
    moved = sum(a.size * a.dtype.itemsize for a in args) + sum(o.size * o.dtype.itemsize for o in outs)
    spaces = [pltpu.SMEM if k in smem else pltpu.HBM if k in hbm else pltpu.VMEM for k in range(len(args))]
    out_spaces = [pltpu.HBM if k in out_hbm else pltpu.VMEM for k in range(len(outs))]
    return pl.pallas_call(
        kernel,
        out_shape=[o if k in out_free else space(o.shape, o.dtype) for k, (o, space) in enumerate(zip(outs, out_spaces))],
        in_specs=[pl.BlockSpec(memory_space=space) for space in spaces],
        out_specs=[pl.BlockSpec(memory_space=space) for space in out_spaces],
        scratch_shapes=list(scratch),
        compiler_params=pltpu.CompilerParams(vmem_limit_bytes=VMEM),
        cost_estimate=pl.CostEstimate(flops=flops, bytes_accessed=moved, transcendentals=0),
    )(*[placed(a, space, k in free) for k, (a, space) in enumerate(zip(args, spaces))])


def placed(value, space, free=False):
    return value if free or space is pltpu.SMEM else pltpu.with_memory_space_constraint(value, space)


def shape(dims, dtype):
    return jax.ShapeDtypeStruct(dims, dtype)


def nt(a, b):
    return lax.dot_general(a, b, (((1,), (1,)), ((), ())), preferred_element_type=F32)


def nn(a, b):
    return jnp.dot(a, b, preferred_element_type=F32)


def iota(dims, axis):
    return lax.broadcasted_iota(I32, dims, axis)


def onehot(mask):
    return jnp.where(mask, 1.0, 0.0).astype(BF16)


def to_col(row):
    return jnp.transpose(jnp.broadcast_to(row, (LANES, row.shape[1])))


def to_row(col):
    return jnp.transpose(jnp.broadcast_to(col, (col.shape[0], LANES)))[0:1, :]


def id_col(ids):
    return to_col(ids.astype(F32))[:, 0:1].astype(I32)


def ranks_of(label, owners, owned):
    rows = label.shape[1]
    start = iota((owners, rows), 0) * owned
    mine = (label >= start) & (label < start + owned)
    before = onehot(iota((rows, rows), 0) <= iota((rows, rows), 1))
    running = nn(onehot(mine), before)
    return mine, jnp.sum(jnp.where(mine, running, 0.0), axis=0, keepdims=True) - 1.0


def slot_of(mine, rank, stride):
    owner = jnp.sum(jnp.where(mine, iota(mine.shape, 0).astype(F32), 0.0), axis=0, keepdims=True)
    return (owner * stride + rank).astype(I32)


def pack_kernel(owners, owned, capacity, label_ref, feat_ref, send_ref, label_buf, feat_buf, send_buf, sems):
    slots, width = send_buf.shape
    rows = label_buf.shape[1]
    stride = slots // owners
    labels = pltpu.make_async_copy(label_ref, label_buf, sems.at[0])
    feats = pltpu.make_async_copy(feat_ref, feat_buf, sems.at[1])
    labels.start()
    feats.start()
    labels.wait()
    label = label_buf[...]
    mine, rank = ranks_of(label, owners, owned)
    slot = slot_of(mine, rank, stride)
    value = jnp.where(mine, (label - iota((owners, rows), 0) * owned + 1).astype(F32), 0.0)
    high = jnp.floor(value * (1.0 / 32.0))
    low = value - 32.0 * high
    place = onehot(to_col(rank)[:, 0:1] == iota((rows, LANES), 1).astype(F32))
    ids = jnp.concatenate(
        [nn(high.astype(BF16), place), nn(low.astype(BF16), place), jnp.zeros((owners, width - 2 * LANES), F32)], axis=1
    ).astype(BF16)
    feats.wait()
    half = slots // 2
    copies = []
    for k in range(2):
        at = slice(k * half, (k + 1) * half)
        spot = iota((half, rows), 0) + k * half
        last = iota((half, owners), 0) + k * half == iota((half, owners), 1) * stride + capacity
        send_buf[at, :] = (nn(onehot(spot == slot), feat_buf[...]) + nn(onehot(last), ids)).astype(BF16)
        copies.append(pltpu.make_async_copy(send_buf.at[at, :], send_ref.at[at, :], sems.at[2 + k]))
        copies[k].start()
    for c in copies:
        c.wait()


def split_kernel(self_ref, neg_ref, old_ref, bank_ref, neg_col_ref, old_col_ref, held_ref, parts_ref, bank_buf, sem):
    owned, width = bank_buf.shape
    negs = neg_ref.shape[1]
    load = pltpu.make_async_copy(bank_ref, bank_buf, sem)
    load.start()
    me = self_ref[0]
    wanted = neg_ref[pl.ds(me, 1), :] - me * owned
    wanted = jnp.concatenate([wanted] * (LANES // negs), axis=1)
    neg_col = id_col(wanted)[0:negs, :]
    neg_col_ref[...] = jnp.broadcast_to(neg_col, neg_col_ref.shape)
    same = neg_col == iota((negs, owned), 1)
    old = jnp.sum(jnp.where(same, old_ref[...], 0.0), axis=1, keepdims=True)
    old_col_ref[...] = jnp.broadcast_to(old, old_col_ref.shape)
    pick = onehot(same)
    load.wait()
    bank = bank_buf[...]
    high = bank.astype(BF16)
    rest = bank - high.astype(F32)
    middle = rest.astype(BF16)
    low = (rest - middle.astype(F32)).astype(BF16)
    parts_ref[:, 0:width] = high
    parts_ref[:, width : 2 * width] = middle
    if parts_ref.shape[1] > 2 * width:
        parts_ref[:, 2 * width :] = low
    held_ref[...] = nn(pick, high) + nn(pick, middle) + nn(pick, low)


def blend(bank, sums, counts):
    safe = jnp.maximum(counts, 1.0)
    return jnp.where(counts > 0, 0.5 * bank + 0.5 * sums / safe, bank)


def mean_kernel(owners, capacity, after_ref, neg_ref, held_ref, parts_ref, got_ref, ids_ref, new_ref, pack_ref, rows_ref):
    owned = parts_ref.shape[0]
    negs, width = held_ref.shape
    sent_rows = got_ref.shape[0]
    stride = sent_rows // owners
    slots = rows_ref.shape[0]
    keep = slots // owners
    last = iota((owners, sent_rows), 1) == iota((owners, sent_rows), 0) * stride + capacity
    sent = nn(onehot(last), got_ref[:, 0 : 2 * LANES]).astype(BF16)
    place = iota((LANES, slots), 1).astype(F32)
    within = place - keep * jnp.floor((place + 0.5) * (1.0 / keep))
    spread = onehot(within == iota((LANES, slots), 0).astype(F32))
    wide = 32.0 * nn(sent[:, 0:LANES], spread) + nn(sent[:, LANES:], spread)
    first = iota((owners, slots), 0) * keep
    spot = iota((owners, slots), 1)
    ids = jnp.sum(jnp.where((spot >= first) & (spot < first + keep), wide, 0.0), axis=0, keepdims=True)
    ids = jnp.where(ids > 0.5, ids - 1.0, float(owned)).astype(I32)
    ids_ref[...] = ids
    for b in range(owners if keep < stride else 0):
        rows_ref[b * keep : (b + 1) * keep, :] = got_ref[b * stride : b * stride + keep, :]
    if keep == stride:
        rows_ref[...] = got_ref[...]
    got = rows_ref[...]
    col = id_col(ids)
    parts = 3
    block = slots // parts if slots % (16 * parts) == 0 else slots
    squares = []
    for k in range(slots // block):
        at = slice(k * block, (k + 1) * block)
        picked = nn(onehot(iota((block, owned), 1) == col[at]), parts_ref[...])
        bank = functools.reduce(jnp.add, [picked[:, j : j + width] for j in range(0, picked.shape[1], width)])
        same = jnp.where(col[at] == ids, 1.0, 0.0)
        new = blend(bank, nn(same.astype(BF16), got), jnp.sum(same, axis=1, keepdims=True))
        new_ref[at, :] = new
        differ = got[at].astype(F32) - new
        squares.append(jnp.sum(differ * differ, axis=1, keepdims=True))
    squared = to_row(jnp.concatenate(squares, axis=0))
    same = jnp.where(neg_ref[:, 0:1] == ids, 1.0, 0.0)
    pack_ref[0:negs, :] = blend(held_ref[...], nn(same.astype(BF16), got), jnp.sum(same, axis=1, keepdims=True))
    for k in range(-(-slots // width)):
        piece = squared[:, k * width : min((k + 1) * width, slots)]
        pack_ref[negs + k : negs + k + 1, 0 : piece.shape[1]] = piece


def concentration(same, dist, old):
    counts = jnp.sum(jnp.where(same, 1.0, 0.0), axis=1, keepdims=True)
    total = jnp.sum(jnp.where(same, dist, 0.0), axis=1, keepdims=True)
    safe = jnp.maximum(counts, 1.0)
    return jnp.where(counts > 0, total / (safe * jnp.log(safe + 10.0)), old)


def neg_kernel(self_ref, ids_ref, neg_ref, old_ref, pack_ref, other_ref, full_ref, own_ref, dist_ref):
    slots, width = ids_ref.shape[1], pack_ref.shape[1]
    negs = neg_ref.shape[0]
    half = negs // 2
    pieces = []
    for k in range(-(-slots // width)):
        part = pack_ref[negs + k : negs + k + 1, :] + other_ref[negs + k : negs + k + 1, :]
        pieces.append(part[:, 0 : min(width, slots - k * width)])
    dist = jnp.sqrt(jnp.concatenate(pieces, axis=1) + 0.25)
    dist_ref[...] = dist
    conc = concentration(neg_ref[:, 0:1] == ids_ref[...], dist, old_ref[:, 0:1])
    mine = (pack_ref[0:negs, :] / conc).astype(BF16)
    other = (other_ref[0:negs, :] / conc).astype(BF16)
    full_ref[:, 0:width] = mine
    full_ref[:, width:] = other
    first = self_ref[1] == 0
    own_ref[:, 0:width] = jnp.where(first, mine[0:half], mine[half:])
    own_ref[:, width:] = jnp.where(first, other[0:half], other[half:])


def scale_kernel(capacity, ids_ref, new_ref, dist_ref, out_ref, buf, sems):
    owners = buf.shape[0]
    stride = new_ref.shape[0] // owners
    ids, dist = ids_ref[...], dist_ref[...]
    col = id_col(ids)
    copies = []
    half = owners // 2
    for k in range(2):
        at = slice(k * half * stride, (k + 1) * half * stride)
        scaled = new_ref[at, :] / concentration(col[at] == ids, dist, 1.0)
        for b in range(half):
            buf[k * half + b] = scaled[b * stride : b * stride + capacity].astype(BF16)
        copies.append(
            pltpu.make_async_copy(buf.at[pl.ds(k * half, half)], out_ref.at[pl.ds(k * half, half)], sems.at[k])
        )
        copies[k].start()
    for c in copies:
        c.wait()


def join_kernel(*refs):
    pieces, joined = refs[1:-2], refs[-2]
    at = 0
    for p in pieces:
        joined[at : at + p.shape[0], :] = p[...]
        at += p.shape[0]


def owner_kernel(ids_ref, dist_ref, got_ref, bank_ref, old_ref, new_ref, conc_ref):
    block = bank_ref.shape[0]
    slots = got_ref.shape[0]
    base = pl.program_id(0) * block
    same = jnp.where(iota((block, slots), 0) + base == ids_ref[...], 1.0, 0.0)
    sums = nn(same.astype(BF16), got_ref[...])
    new_ref[...] = blend(bank_ref[...], sums, jnp.sum(same, axis=1, keepdims=True))
    turned = iota((slots, block), 1) + base == id_col(ids_ref[...])
    counts = jnp.sum(jnp.where(turned, 1.0, 0.0), axis=0, keepdims=True)
    total = jnp.sum(jnp.where(turned, to_col(dist_ref[...])[:, 0:1], 0.0), axis=0, keepdims=True)
    safe = jnp.maximum(counts, 1.0)
    conc_ref[...] = jnp.where(counts > 0, total / (safe * jnp.log(safe + 10.0)), old_ref[...])


def owner_call(ids, dist, got, bank, old):
    owned, width = bank.shape
    slots = got.shape[0]
    block = 256
    whole = lambda k: (0, 0)
    return pl.pallas_call(
        owner_kernel,
        grid=(owned // block,),
        in_specs=[
            pl.BlockSpec((1, slots), whole),
            pl.BlockSpec((1, slots), whole),
            pl.BlockSpec((slots, width), whole),
            pl.BlockSpec((block, width), lambda k: (k, 0)),
            pl.BlockSpec((1, block), lambda k: (0, k)),
        ],
        out_specs=[pl.BlockSpec((block, width), lambda k: (k, 0)), pl.BlockSpec((1, block), lambda k: (0, k))],
        out_shape=[shape((owned, width), F32), shape((1, owned), F32)],
        compiler_params=pltpu.CompilerParams(vmem_limit_bytes=VMEM),
        cost_estimate=pl.CostEstimate(flops=10**12, bytes_accessed=8 * owned * width, transcendentals=0),
    )(ids, dist, got, placed(bank, pltpu.HBM), placed(old, pltpu.HBM))


def flash_kernel(owners, owned, capacity, after_ref, label_ref, mine_ref, other_ref, *refs):
    parts, (keep_ref, stats_ref, send_ref, slot_ref, copy_ref) = refs[:-5], refs[-5:]
    width = mine_ref.shape[1]
    slot = slot_of(*ranks_of(label_ref[...], owners, owned), capacity)
    slot_ref[...] = to_col(slot.astype(F32)).astype(I32)
    copy_ref[...] = mine_ref[...]
    rows = mine_ref.shape[0]
    mine, other = mine_ref[...], other_ref[...]
    logits = [nt(mine, p[:, 0:width]) + nt(other, p[:, width:]) for p in parts]
    top = functools.reduce(jnp.maximum, [jnp.max(l, axis=1, keepdims=True) for l in logits])
    total = jnp.zeros((rows, 1), F32)
    grad = jnp.zeros((rows, 2 * width), F32)
    for l, p in zip(logits, parts):
        weight = jnp.exp(l - top)
        total = total + jnp.sum(weight, axis=1, keepdims=True)
        grad = grad + nn(weight.astype(BF16), p[...])
    keep_ref[...] = grad[:, 0:width]
    send_ref[0:rows, :] = grad[:, width:]
    stats = jnp.concatenate([to_row(top), to_row(total)], axis=0)
    stats_ref[0:2, :] = stats
    send_ref[rows : rows + 2, 0:rows] = stats


def positive_kernel(slot_ref, query_ref, back_ref, rows_ref, part_ref):
    rows, slots = query_ref.shape[0], back_ref.shape[0]
    found = nn(onehot(iota((rows, slots), 1) == slot_ref[:, 0:1]), back_ref[...])
    rows_ref[...] = found.astype(BF16)
    part = to_row(jnp.sum(query_ref[...].astype(F32) * found, axis=1, keepdims=True))
    part_ref[...] = jnp.broadcast_to(part, part_ref.shape)


def final_kernel(self_ref, part_ref, far_ref, stats_ref, keep_ref, sent_ref, rows_ref, loss_ref, grad_ref):
    rows = keep_ref.shape[0]
    first = self_ref[1] == 0
    here, there = stats_ref[0:2, :], sent_ref[rows : rows + 2, 0:rows]
    low = jnp.where(first, here, there)
    high = jnp.where(first, there, here)
    positive = part_ref[0:1, :] + far_ref[0:1, :]
    top = jnp.maximum(jnp.maximum(low[0:1], high[0:1]), positive)
    exppos = jnp.exp(positive - top)
    total = low[1:2] * jnp.exp(low[0:1] - top) + high[1:2] * jnp.exp(high[0:1] - top) + exppos
    loss_ref[...] = jnp.log(total) + top - positive
    mine = to_col(jnp.exp(here[0:1] - top) / total)[:, 0:1]
    other = to_col(jnp.exp(there[0:1] - top) / total)[:, 0:1]
    pull = to_col(exppos / total - 1.0)[:, 0:1]
    grad_ref[...] = keep_ref[...] * mine + sent_ref[0:rows, :] * other + pull * rows_ref[...].astype(F32)


def swap(value):
    return lax.ppermute(value, "mp", [(0, 1), (1, 0)])


def hop(value, count, bits):
    return lax.ppermute(value, "dp", [(k, k ^ bits) for k in range(count)])


def two_hop(value, count, bits):
    return lax.ppermute(
        value, ("dp", "mp"), [(2 * k + c, 2 * (k ^ bits[c]) + c) for k in range(count) for c in range(2)]
    )


def join(value, pieces):
    rows = sum(p.shape[0] for p in pieces)
    return pl.pallas_call(
        join_kernel,
        out_shape=[pltpu.VMEM((rows, pieces[0].shape[1]), BF16), pltpu.HBM(value.shape, value.dtype)],
        in_specs=[pl.BlockSpec(memory_space=pltpu.HBM)] + [pl.BlockSpec(memory_space=pltpu.VMEM) for _ in pieces],
        out_specs=[pl.BlockSpec(memory_space=pltpu.VMEM), pl.BlockSpec(memory_space=pltpu.HBM)],
        input_output_aliases={0: 1},
        compiler_params=pltpu.CompilerParams(vmem_limit_bytes=VMEM),
    )(placed(value, pltpu.HBM), *[placed(p, pltpu.VMEM) for p in pieces])


def body(features, labels, queries, bank, old_conc, neg_index):
    count = lax.axis_size("dp")
    me, core = lax.axis_index("dp"), lax.axis_index("mp")
    owned, width = bank.shape
    rows = features.shape[0]
    capacity = 3 * rows // count
    stride = 8 * -(-(capacity + 1) // 8)
    slots = count * stride
    negs = neg_index.shape[0] // count
    half = negs // 2
    place = jnp.stack([me, core]).astype(I32)
    loads = [pltpu.VMEM((1, rows), I32), pltpu.VMEM((rows, width), BF16)]

    label_row = labels.reshape(1, rows)
    (send,) = call(
        functools.partial(pack_kernel, count, owned, capacity),
        (shape((slots, width), BF16),),
        label_row, features, flops=2 * slots * rows * width, hbm=(0, 1), out_hbm=(0,),
        scratch=[*loads, pltpu.VMEM((slots, width), BF16), pltpu.SemaphoreType.DMA((4,))],
    )
    query_far = swap(queries)
    got = lax.all_to_all(send.reshape(count, stride, width), "dp", split_axis=0, concat_axis=0)
    got = got.reshape(slots, width)

    neg_col, old_col, held, parts = call(
        split_kernel,
        (shape((negs, LANES), I32), shape((negs, LANES), F32), shape((negs, width), F32), shape((owned, 2 * width), BF16)),
        place, neg_index.reshape(count, negs), old_conc.reshape(1, owned), bank, smem=(0,), hbm=(3,), free=(1, 2),
        scratch=[pltpu.VMEM((owned, width), F32), pltpu.SemaphoreType.DMA],
    )
    sent_rows = slots
    slots = count * capacity if capacity % 16 == 0 else slots
    extra = 8 * -(-slots // (8 * width))
    ids, new, pack, got = call(
        functools.partial(mean_kernel, count, capacity),
        (shape((1, slots), I32), shape((slots, width), F32), shape((negs + extra, width), F32), shape((slots, width), BF16)),
        query_far, neg_col, held, parts, got, flops=8 * slots * owned * width, hbm=(0,),
    )
    full, own, dist = call(
        neg_kernel,
        (shape((negs, 2 * width), BF16), shape((half, 2 * width), BF16), shape((1, slots), F32)),
        place, ids, neg_col, old_col, pack, swap(pack), smem=(0,),
    )
    (scaled,) = call(
        functools.partial(scale_kernel, capacity),
        (shape((count, capacity, width), BF16),),
        ids, new, dist, out_hbm=(0,),
        scratch=[pltpu.VMEM((count, capacity, width), BF16), pltpu.SemaphoreType.DMA((2,))],
    )
    step = count // 4
    line = [own, two_hop(full, count, (step, 2 * step)), hop(own, count, 3 * step)]
    joined, scaled = join(scaled, line)
    pieces = [joined]
    while step > 1:
        few = min(4, step)
        step //= few
        pieces = [joined] + [hop(joined, count, step * k) for k in range(1, few)]
        if step > 1:
            joined = jnp.concatenate(pieces, axis=0)
    back = lax.all_to_all(scaled, "dp", split_axis=0, concat_axis=0)
    new_bank, new_conc = owner_call(ids, dist, got, bank, old_conc.reshape(1, owned))
    keep, stats, sent, slot, query = call(
        functools.partial(flash_kernel, count, owned, capacity),
        (
            shape((rows, width), F32), shape((8, rows), F32), shape((rows + 8, width), F32),
            shape((rows, LANES), I32), shape((rows, width), BF16),
        ),
        new_conc, label_row, queries, query_far, *pieces,
        flops=8 * rows * half * count * width, hbm=(0,), free=range(1, 99),
    )
    sent = swap(sent)
    found, part = call(
        positive_kernel,
        (shape((rows, width), BF16), shape((8, rows), F32)),
        slot, query, back.reshape(count * capacity, width), flops=2 * slots * rows * width,
    )
    loss, grad = call(
        final_kernel,
        (shape((1, rows), F32), shape((rows, width), F32)),
        place, part, swap(part), stats, keep, sent, found, smem=(0,), out_free=(0, 1),
    )
    return (new_bank, new_conc.reshape(owned), loss.reshape(rows), grad)


def solution(mesh):
    placed = (P("dp", "mp"), P("dp"), P("dp", "mp"), P("dp", "mp"), P("dp"), P())
    return jax.shard_map(
        body,
        mesh=mesh,
        in_specs=placed,
        out_specs=(P("dp", "mp"), P("dp"), P("dp"), P("dp", "mp")),
        check_vma=False,
    )
```

```python
import functools

import jax
import jax.numpy as jnp
from jax import lax
from jax.experimental import pallas as pl
from jax.experimental.pallas import tpu as pltpu
from jax.sharding import PartitionSpec as P

F32 = jnp.float32
BF16 = jnp.bfloat16
I32 = jnp.int32
LANES = 128
VMEM = 24 * 2**20


def call(kernel, outs, *args, flops=0, smem=(), hbm=(), out_hbm=(), free=(), out_free=(), scratch=()):
    moved = sum(a.size * a.dtype.itemsize for a in args) + sum(o.size * o.dtype.itemsize for o in outs)
    spaces = [pltpu.SMEM if k in smem else pltpu.HBM if k in hbm else pltpu.VMEM for k in range(len(args))]
    out_spaces = [pltpu.HBM if k in out_hbm else pltpu.VMEM for k in range(len(outs))]
    return pl.pallas_call(
        kernel,
        out_shape=[o if k in out_free else space(o.shape, o.dtype) for k, (o, space) in enumerate(zip(outs, out_spaces))],
        in_specs=[pl.BlockSpec(memory_space=space) for space in spaces],
        out_specs=[pl.BlockSpec(memory_space=space) for space in out_spaces],
        scratch_shapes=list(scratch),
        name=getattr(kernel, "func", kernel).__name__,
        compiler_params=pltpu.CompilerParams(vmem_limit_bytes=VMEM),
        cost_estimate=pl.CostEstimate(flops=flops, bytes_accessed=moved, transcendentals=0),
    )(*[placed(a, space, k in free) for k, (a, space) in enumerate(zip(args, spaces))])


def placed(value, space, free=False):
    return value if free or space is pltpu.SMEM else pltpu.with_memory_space_constraint(value, space)


def shape(dims, dtype):
    return jax.ShapeDtypeStruct(dims, dtype)


def nt(a, b):
    return lax.dot_general(a, b, (((1,), (1,)), ((), ())), preferred_element_type=F32)


def nn(a, b):
    return jnp.dot(a, b, preferred_element_type=F32)


def iota(dims, axis):
    return lax.broadcasted_iota(I32, dims, axis)


def onehot(mask):
    return jnp.where(mask, 1.0, 0.0).astype(BF16)


def to_col(row):
    return jnp.transpose(jnp.broadcast_to(row, (LANES, row.shape[1])))


def to_row(col):
    return jnp.transpose(jnp.broadcast_to(col, (col.shape[0], LANES)))[0:1, :]


def id_col(ids):
    return to_col(ids.astype(F32))[:, 0:1].astype(I32)


def ranks_of(label, owners, owned):
    rows = label.shape[1]
    start = iota((owners, rows), 0) * owned
    mine = (label >= start) & (label < start + owned)
    before = onehot(iota((rows, rows), 0) <= iota((rows, rows), 1))
    running = nn(onehot(mine), before)
    return mine, jnp.sum(jnp.where(mine, running, 0.0), axis=0, keepdims=True) - 1.0


def slot_of(mine, rank, stride):
    owner = jnp.sum(jnp.where(mine, iota(mine.shape, 0).astype(F32), 0.0), axis=0, keepdims=True)
    return (owner * stride + rank).astype(I32)


def pack_kernel(owners, owned, stride, label_ref, feat_ref, send_ref, label_buf, feat_buf, send_buf, sems):
    rows, width = feat_buf.shape
    block = send_buf.shape[0] // owners
    labels = pltpu.make_async_copy(label_ref, label_buf, sems.at[0])
    feats = pltpu.make_async_copy(feat_ref, feat_buf, sems.at[1])
    labels.start()
    feats.start()
    labels.wait()
    label = label_buf[...]
    mine, rank = ranks_of(label, owners, owned)
    slot = slot_of(mine, rank, stride)
    value = jnp.where(mine, (label - iota((owners, rows), 0) * owned + 1).astype(F32), 0.0)
    high = jnp.floor(value * (1.0 / 32.0))
    value = jnp.concatenate([high, value - 32.0 * high], axis=0).astype(BF16)
    place = onehot(to_col(rank)[:, 0:1] == iota((rows, LANES), 1).astype(F32))
    ids = nn(value, place).astype(BF16)
    row, part = iota((8 * owners, 2 * owners), 0), iota((8 * owners, 2 * owners), 1)
    ids = nn(onehot(row == jnp.where(part < owners, 8 * part, 8 * (part - owners) + 1)), ids).astype(BF16)
    feats.wait()
    half = owners // 2
    copies = []
    for k in range(2):
        spot = iota((half * stride, rows), 0) + k * half * stride
        picked = nn(onehot(spot == slot), feat_buf[...]).astype(BF16)
        for b in range(half):
            at = (k * half + b) * block
            for j in range(width // LANES):
                piece = picked[b * stride : (b + 1) * stride, j * LANES : (j + 1) * LANES]
                send_buf[at + j * stride : at + (j + 1) * stride, :] = piece
            send_buf[at + block - 8 : at + block, :] = ids[(k * half + b) * 8 : (k * half + b + 1) * 8, :]
        at = slice(k * half * block, (k + 1) * half * block)
        copies.append(pltpu.make_async_copy(send_buf.at[at, :], send_ref.at[at, :], sems.at[2 + k]))
        copies[k].start()
    for c in copies:
        c.wait()


def split_kernel(self_ref, neg_ref, old_ref, bank_ref, neg_col_ref, old_col_ref, held_ref, parts_ref, bank_buf, sem):
    owned, width = bank_buf.shape
    negs = neg_ref.shape[1]
    load = pltpu.make_async_copy(bank_ref, bank_buf, sem)
    load.start()
    me = self_ref[0]
    wanted = neg_ref[pl.ds(me, 1), :] - me * owned
    wanted = jnp.concatenate([wanted] * (LANES // negs), axis=1)
    neg_col = id_col(wanted)[0:negs, :]
    neg_col_ref[...] = jnp.broadcast_to(neg_col, neg_col_ref.shape)
    same = neg_col == iota((negs, owned), 1)
    old = jnp.sum(jnp.where(same, old_ref[...], 0.0), axis=1, keepdims=True)
    old_col_ref[...] = jnp.broadcast_to(old, old_col_ref.shape)
    pick = onehot(same)
    load.wait()
    bank = bank_buf[...]
    high = bank.astype(BF16)
    rest = bank - high.astype(F32)
    middle = rest.astype(BF16)
    low = (rest - middle.astype(F32)).astype(BF16)
    parts_ref[:, 0:width] = high
    parts_ref[:, width : 2 * width] = middle
    if parts_ref.shape[1] > 2 * width:
        parts_ref[:, 2 * width :] = low
    held_ref[...] = nn(pick, high) + nn(pick, middle) + nn(pick, low)


def blend(bank, sums, counts):
    safe = jnp.maximum(counts, 1.0)
    return jnp.where(counts > 0, 0.5 * bank + 0.5 * sums / safe, bank)


def mean_kernel(owners, after_ref, neg_ref, held_ref, parts_ref, got_ref, ids_ref, new_ref, pack_ref, rows_ref):
    owned = parts_ref.shape[0]
    negs, width = held_ref.shape
    slots = rows_ref.shape[0]
    keep = slots // owners
    block = got_ref.shape[0] // owners
    stride = (block - 8) // (width // LANES)
    spot, part = iota((2 * owners, got_ref.shape[0]), 1), iota((2 * owners, got_ref.shape[0]), 0)
    first = jnp.where(part < owners, part * block, (part - owners) * block + 1) + block - 8
    sent = nn(onehot(spot == first), got_ref[...]).astype(BF16)
    place = iota((LANES, slots), 1).astype(F32)
    within = place - keep * jnp.floor((place + 0.5) * (1.0 / keep))
    spread = onehot(within == iota((LANES, slots), 0).astype(F32))
    wide = 32.0 * nn(sent[0:owners], spread) + nn(sent[owners:], spread)
    first = iota((owners, slots), 0) * keep
    spot = iota((owners, slots), 1)
    ids = jnp.sum(jnp.where((spot >= first) & (spot < first + keep), wide, 0.0), axis=0, keepdims=True)
    ids = jnp.where(ids > 0.5, ids - 1.0, float(owned)).astype(I32)
    ids_ref[...] = ids
    for b in range(owners):
        for j in range(width // LANES):
            at = b * block + j * stride
            rows_ref[b * keep : (b + 1) * keep, j * LANES : (j + 1) * LANES] = got_ref[at : at + keep, :]
    got = rows_ref[...]
    col = id_col(ids)
    parts = 3
    block = slots // parts if slots % (16 * parts) == 0 else slots
    squares = []
    for k in range(slots // block):
        at = slice(k * block, (k + 1) * block)
        picked = nn(onehot(iota((block, owned), 1) == col[at]), parts_ref[...])
        bank = functools.reduce(jnp.add, [picked[:, j : j + width] for j in range(0, picked.shape[1], width)])
        same = jnp.where(col[at] == ids, 1.0, 0.0)
        new = blend(bank, nn(same.astype(BF16), got), jnp.sum(same, axis=1, keepdims=True))
        new_ref[at, :] = new
        differ = got[at].astype(F32) - new
        squares.append(jnp.sum(differ * differ, axis=1, keepdims=True))
    squared = to_row(jnp.concatenate(squares, axis=0))
    same = jnp.where(neg_ref[:, 0:1] == ids, 1.0, 0.0)
    pack_ref[0:negs, :] = blend(held_ref[...], nn(same.astype(BF16), got), jnp.sum(same, axis=1, keepdims=True))
    for k in range(-(-slots // width)):
        piece = squared[:, k * width : min((k + 1) * width, slots)]
        pack_ref[negs + k : negs + k + 1, 0 : piece.shape[1]] = piece


def concentration(same, dist, old):
    counts = jnp.sum(jnp.where(same, 1.0, 0.0), axis=1, keepdims=True)
    total = jnp.sum(jnp.where(same, dist, 0.0), axis=1, keepdims=True)
    safe = jnp.maximum(counts, 1.0)
    return jnp.where(counts > 0, total / (safe * jnp.log(safe + 10.0)), old)


def neg_kernel(self_ref, ids_ref, neg_ref, old_ref, pack_ref, other_ref, full_ref, own_ref, dist_ref):
    slots, width = ids_ref.shape[1], pack_ref.shape[1]
    negs = neg_ref.shape[0]
    half = negs // 2
    pieces = []
    for k in range(-(-slots // width)):
        part = pack_ref[negs + k : negs + k + 1, :] + other_ref[negs + k : negs + k + 1, :]
        pieces.append(part[:, 0 : min(width, slots - k * width)])
    dist = jnp.sqrt(jnp.concatenate(pieces, axis=1) + 0.25)
    dist_ref[...] = dist
    conc = concentration(neg_ref[:, 0:1] == ids_ref[...], dist, old_ref[:, 0:1])
    mine = (pack_ref[0:negs, :] / conc).astype(BF16)
    other = (other_ref[0:negs, :] / conc).astype(BF16)
    full_ref[:, 0:width] = mine
    full_ref[:, width:] = other
    first = self_ref[1] == 0
    own_ref[:, 0:width] = jnp.where(first, mine[0:half], mine[half:])
    own_ref[:, width:] = jnp.where(first, other[0:half], other[half:])


def scale_kernel(capacity, ids_ref, new_ref, dist_ref, out_ref, buf, sems):
    owners = buf.shape[0]
    stride = new_ref.shape[0] // owners
    ids, dist = ids_ref[...], dist_ref[...]
    col = id_col(ids)
    copies = []
    half = owners // 2
    for k in range(2):
        at = slice(k * half * stride, (k + 1) * half * stride)
        scaled = new_ref[at, :] / concentration(col[at] == ids, dist, 1.0)
        for b in range(half):
            buf[k * half + b] = scaled[b * stride : b * stride + capacity].astype(BF16)
        copies.append(
            pltpu.make_async_copy(buf.at[pl.ds(k * half, half)], out_ref.at[pl.ds(k * half, half)], sems.at[k])
        )
        copies[k].start()
    for c in copies:
        c.wait()


def join_kernel(*refs):
    pieces, joined = refs[:-1], refs[-1]
    at = 0
    for p in pieces:
        joined[at : at + p.shape[0], :] = p[...]
        at += p.shape[0]


def owner_kernel(ids_ref, dist_ref, got_ref, bank_ref, old_ref, new_ref, conc_ref):
    block = bank_ref.shape[0]
    slots = got_ref.shape[0]
    base = pl.program_id(0) * block
    same = jnp.where(iota((block, slots), 0) + base == ids_ref[...], 1.0, 0.0)
    sums = nn(same.astype(BF16), got_ref[...])
    new_ref[...] = blend(bank_ref[...], sums, jnp.sum(same, axis=1, keepdims=True))
    turned = iota((slots, block), 1) + base == id_col(ids_ref[...])
    counts = jnp.sum(jnp.where(turned, 1.0, 0.0), axis=0, keepdims=True)
    total = jnp.sum(jnp.where(turned, to_col(dist_ref[...])[:, 0:1], 0.0), axis=0, keepdims=True)
    safe = jnp.maximum(counts, 1.0)
    conc_ref[...] = jnp.where(counts > 0, total / (safe * jnp.log(safe + 10.0)), old_ref[...])


def owner_call(ids, dist, got, bank, old):
    owned, width = bank.shape
    slots = got.shape[0]
    block = 256
    whole = lambda k: (0, 0)
    return pl.pallas_call(
        owner_kernel,
        grid=(owned // block,),
        in_specs=[
            pl.BlockSpec((1, slots), whole),
            pl.BlockSpec((1, slots), whole),
            pl.BlockSpec((slots, width), whole),
            pl.BlockSpec((block, width), lambda k: (k, 0)),
            pl.BlockSpec((1, block), lambda k: (0, k)),
        ],
        out_specs=[pl.BlockSpec((block, width), lambda k: (k, 0)), pl.BlockSpec((1, block), lambda k: (0, k))],
        out_shape=[shape((owned, width), F32), shape((1, owned), F32)],
        name="owner_kernel",
        compiler_params=pltpu.CompilerParams(vmem_limit_bytes=VMEM),
        cost_estimate=pl.CostEstimate(flops=10000000000, bytes_accessed=8 * owned * width, transcendentals=0),
    )(ids, dist, got, placed(bank, pltpu.HBM), placed(old, pltpu.HBM))


def flash_kernel(owners, owned, capacity, after_ref, label_ref, mine_ref, other_ref, *refs):
    parts, (keep_ref, stats_ref, send_ref, slot_ref, copy_ref) = refs[:-5], refs[-5:]
    width = mine_ref.shape[1]
    slot = slot_of(*ranks_of(label_ref[...], owners, owned), capacity)
    slot_ref[...] = to_col(slot.astype(F32)).astype(I32)
    copy_ref[...] = mine_ref[...]
    rows = mine_ref.shape[0]
    mine, other = mine_ref[...], other_ref[...]
    logits = [nt(mine, p[:, 0:width]) + nt(other, p[:, width:]) for p in parts]
    top = functools.reduce(jnp.maximum, [jnp.max(l, axis=1, keepdims=True) for l in logits])
    total = jnp.zeros((rows, 1), F32)
    grad = jnp.zeros((rows, 2 * width), F32)
    for l, p in zip(logits, parts):
        weight = jnp.exp(l - top)
        total = total + jnp.sum(weight, axis=1, keepdims=True)
        grad = grad + nn(weight.astype(BF16), p[...])
    keep_ref[...] = grad[:, 0:width]
    send_ref[0:rows, :] = grad[:, width:]
    stats = jnp.concatenate([to_row(top), to_row(total)], axis=0)
    stats_ref[0:2, :] = stats
    send_ref[rows : rows + 2, 0:rows] = stats


def positive_kernel(slot_ref, query_ref, back_ref, rows_ref, part_ref):
    rows, slots = query_ref.shape[0], back_ref.shape[0]
    found = nn(onehot(iota((rows, slots), 1) == slot_ref[:, 0:1]), back_ref[...])
    rows_ref[...] = found.astype(BF16)
    part = to_row(jnp.sum(query_ref[...].astype(F32) * found, axis=1, keepdims=True))
    part_ref[...] = jnp.broadcast_to(part, part_ref.shape)


def final_kernel(self_ref, part_ref, far_ref, stats_ref, keep_ref, sent_ref, rows_ref, loss_ref, grad_ref):
    rows = keep_ref.shape[0]
    first = self_ref[1] == 0
    here, there = stats_ref[0:2, :], sent_ref[rows : rows + 2, 0:rows]
    low = jnp.where(first, here, there)
    high = jnp.where(first, there, here)
    positive = part_ref[0:1, :] + far_ref[0:1, :]
    top = jnp.maximum(jnp.maximum(low[0:1], high[0:1]), positive)
    exppos = jnp.exp(positive - top)
    total = low[1:2] * jnp.exp(low[0:1] - top) + high[1:2] * jnp.exp(high[0:1] - top) + exppos
    loss_ref[...] = jnp.log(total) + top - positive
    mine = to_col(jnp.exp(here[0:1] - top) / total)[:, 0:1]
    other = to_col(jnp.exp(there[0:1] - top) / total)[:, 0:1]
    pull = to_col(exppos / total - 1.0)[:, 0:1]
    grad_ref[...] = keep_ref[...] * mine + sent_ref[0:rows, :] * other + pull * rows_ref[...].astype(F32)


def swap(value):
    return lax.ppermute(value, "mp", [(0, 1), (1, 0)])


def hop(value, count, bits):
    return lax.ppermute(value, "dp", [(k, k ^ bits) for k in range(count)])


def two_hop(value, count, bits):
    return lax.ppermute(
        value, ("dp", "mp"), [(2 * k + c, 2 * (k ^ bits[c]) + c) for k in range(count) for c in range(2)]
    )


def join(value, pieces):
    rows = sum(p.shape[0] for p in pieces)
    return pl.pallas_call(
        join_kernel,
        out_shape=[pltpu.VMEM((rows, pieces[0].shape[1]), BF16), pltpu.HBM(value.shape, value.dtype)],
        in_specs=[pl.BlockSpec(memory_space=pltpu.HBM)] + [pl.BlockSpec(memory_space=pltpu.VMEM) for _ in pieces],
        out_specs=[pl.BlockSpec(memory_space=pltpu.VMEM), pl.BlockSpec(memory_space=pltpu.HBM)],
        input_output_aliases={0: 1},
        name="join_kernel",
        compiler_params=pltpu.CompilerParams(vmem_limit_bytes=VMEM),
    )(placed(value, pltpu.HBM), *[placed(p, pltpu.VMEM) for p in pieces])


def body(features, labels, queries, bank, old_conc, neg_index):
    count = lax.axis_size("dp")
    me, core = lax.axis_index("dp"), lax.axis_index("mp")
    owned, width = bank.shape
    rows = features.shape[0]
    capacity = 3 * rows // count
    stride = 8 * -(-capacity // 8)
    block = stride * (width // LANES) + 8
    slots = count * stride
    negs = neg_index.shape[0] // count
    half = negs // 2
    place = jnp.stack([me, core]).astype(I32)
    loads = [pltpu.VMEM((1, rows), I32), pltpu.VMEM((rows, width), BF16)]

    label_row = labels.reshape(1, rows)
    (send,) = call(
        functools.partial(pack_kernel, count, owned, stride),
        (shape((count * block, LANES), BF16),),
        label_row, features, flops=2 * slots * rows * width, hbm=(0, 1), out_hbm=(0,),
        scratch=[*loads, pltpu.VMEM((count * block, LANES), BF16), pltpu.SemaphoreType.DMA((4,))],
    )
    query_far = swap(queries)
    got = lax.all_to_all(send.reshape(count, block, LANES), "dp", split_axis=0, concat_axis=0)
    got = got.reshape(count * block, LANES)

    neg_col, old_col, held, parts = call(
        split_kernel,
        (shape((negs, LANES), I32), shape((negs, LANES), F32), shape((negs, width), F32), shape((owned, 2 * width), BF16)),
        place, neg_index.reshape(count, negs), old_conc.reshape(1, owned), bank, smem=(0,), hbm=(3,), free=(1, 2),
        scratch=[pltpu.VMEM((owned, width), F32), pltpu.SemaphoreType.DMA],
    )
    extra = 8 * -(-slots // (8 * width))
    ids, new, pack, got = call(
        functools.partial(mean_kernel, count),
        (shape((1, slots), I32), shape((slots, width), F32), shape((negs + extra, width), F32), shape((slots, width), BF16)),
        query_far, neg_col, held, parts, got, flops=8 * slots * owned * width, hbm=(0,),
    )
    full, own, dist = call(
        neg_kernel,
        (shape((negs, 2 * width), BF16), shape((half, 2 * width), BF16), shape((1, slots), F32)),
        place, ids, neg_col, old_col, pack, swap(pack), smem=(0,),
    )
    (scaled,) = call(
        functools.partial(scale_kernel, capacity),
        (shape((count, capacity, width), BF16),),
        ids, new, dist, out_hbm=(0,), flops=1000000000000,
        scratch=[pltpu.VMEM((count, capacity, width), BF16), pltpu.SemaphoreType.DMA((2,))],
    )
    step = count // 4
    line = [own, two_hop(full, count, (step, 2 * step)), hop(own, count, 3 * step)]
    (joined,) = call(join_kernel, (shape((sum(p.shape[0] for p in line), 2 * width), BF16),), *line)
    pieces = [joined]
    while step > 1:
        few = min(4, step)
        step //= few
        pieces = [joined] + [hop(joined, count, step * k) for k in range(1, few)]
        if step > 1:
            joined = jnp.concatenate(pieces, axis=0)
    back = lax.all_to_all(scaled, "dp", split_axis=0, concat_axis=0)
    new_bank, new_conc = owner_call(ids, dist, got, bank, old_conc.reshape(1, owned))
    keep, stats, sent, slot, query = call(
        functools.partial(flash_kernel, count, owned, capacity),
        (
            shape((rows, width), F32), shape((8, rows), F32), shape((rows + 8, width), F32),
            shape((rows, LANES), I32), shape((rows, width), BF16),
        ),
        new_conc, label_row, queries, query_far, *pieces,
        flops=8 * rows * half * count * width, hbm=(0,), free=range(1, 99),
    )
    sent = swap(sent)
    found, part = call(
        positive_kernel,
        (shape((rows, width), BF16), shape((8, rows), F32)),
        slot, query, back.reshape(count * capacity, width), flops=2 * slots * rows * width,
    )
    loss, grad = call(
        final_kernel,
        (shape((1, rows), F32), shape((rows, width), F32)),
        place, part, swap(part), stats, keep, sent, found, smem=(0,), out_free=(0, 1),
    )
    return (new_bank, new_conc.reshape(owned), loss.reshape(rows), grad)


def solution(mesh):
    placed = (P("dp", "mp"), P("dp"), P("dp", "mp"), P("dp", "mp"), P("dp"), P())
    return jax.shard_map(
        body,
        mesh=mesh,
        in_specs=placed,
        out_specs=(P("dp", "mp"), P("dp"), P("dp"), P("dp", "mp")),
        check_vma=False,
    )
```

```python
import functools

import jax
import jax.numpy as jnp
from jax import lax
from jax.experimental import pallas as pl
from jax.experimental.pallas import tpu as pltpu
from jax.sharding import PartitionSpec as P

F32 = jnp.float32
BF16 = jnp.bfloat16
I32 = jnp.int32
LANES = 128
VMEM = 24 * 2**20


def call(kernel, outs, *args, flops=0, smem=(), hbm=(), out_hbm=(), free=(), out_free=(), scratch=()):
    moved = sum(a.size * a.dtype.itemsize for a in args) + sum(o.size * o.dtype.itemsize for o in outs)
    spaces = [pltpu.SMEM if k in smem else pltpu.HBM if k in hbm else pltpu.VMEM for k in range(len(args))]
    out_spaces = [pltpu.HBM if k in out_hbm else pltpu.VMEM for k in range(len(outs))]
    return pl.pallas_call(
        kernel,
        out_shape=[o if k in out_free else space(o.shape, o.dtype) for k, (o, space) in enumerate(zip(outs, out_spaces))],
        in_specs=[pl.BlockSpec(memory_space=space) for space in spaces],
        out_specs=[pl.BlockSpec(memory_space=space) for space in out_spaces],
        scratch_shapes=list(scratch),
        name=getattr(kernel, "func", kernel).__name__,
        compiler_params=pltpu.CompilerParams(vmem_limit_bytes=VMEM),
        cost_estimate=pl.CostEstimate(flops=flops, bytes_accessed=moved, transcendentals=0),
    )(*[placed(a, space, k in free) for k, (a, space) in enumerate(zip(args, spaces))])


def placed(value, space, free=False):
    return value if free or space is pltpu.SMEM else pltpu.with_memory_space_constraint(value, space)


def shape(dims, dtype):
    return jax.ShapeDtypeStruct(dims, dtype)


def nt(a, b):
    return lax.dot_general(a, b, (((1,), (1,)), ((), ())), preferred_element_type=F32)


def nn(a, b):
    return jnp.dot(a, b, preferred_element_type=F32)


def iota(dims, axis):
    return lax.broadcasted_iota(I32, dims, axis)


def onehot(mask):
    return jnp.where(mask, 1.0, 0.0).astype(BF16)


def to_col(row):
    return jnp.transpose(jnp.broadcast_to(row, (LANES, row.shape[1])))


def to_row(col):
    return jnp.transpose(jnp.broadcast_to(col, (col.shape[0], LANES)))[0:1, :]


def id_col(ids):
    return to_col(ids.astype(F32))[:, 0:1].astype(I32)


def ahead(rows):
    return onehot(iota((rows, rows), 0) <= iota((rows, rows), 1))


def ranks_of(label, owners, owned, before):
    start = iota((owners, label.shape[1]), 0) * owned
    mine = (label >= start) & (label < start + owned)
    running = nn(onehot(mine), before)
    return mine, jnp.sum(jnp.where(mine, running, 0.0), axis=0, keepdims=True) - 1.0


def slot_of(mine, rank, stride):
    owner = jnp.sum(jnp.where(mine, iota(mine.shape, 0).astype(F32), 0.0), axis=0, keepdims=True)
    return (owner * stride + rank).astype(I32)


def pack_kernel(owners, owned, stride, label_ref, feat_ref, send_ref, label_buf, feat_buf, send_buf, sems):
    rows, width = feat_buf.shape
    block = send_buf.shape[0] // owners
    labels = pltpu.make_async_copy(label_ref, label_buf, sems.at[0])
    feats = pltpu.make_async_copy(feat_ref, feat_buf, sems.at[1])
    labels.start()
    feats.start()
    before = ahead(rows)
    labels.wait()
    label = label_buf[...]
    mine, rank = ranks_of(label, owners, owned, before)
    slot = slot_of(mine, rank, stride)
    value = jnp.where(mine, (label - iota((owners, rows), 0) * owned + 1).astype(F32), 0.0)
    high = jnp.floor(value * (1.0 / 32.0))
    value = jnp.concatenate([high, value - 32.0 * high], axis=0).astype(BF16)
    ids = nt(value, onehot(iota((LANES, rows), 0).astype(F32) == rank))
    feats.wait()
    chunks = 4
    part = owners // chunks
    copies = []
    row = iota((8, LANES), 0)
    for k in range(chunks):
        spot = iota((part * stride, rows), 0) + k * part * stride
        picked = nn(onehot(spot == slot), feat_buf[...]).astype(BF16)
        for c in range(part):
            b = k * part + c
            for j in range(width // LANES):
                piece = picked[c * stride : (c + 1) * stride, j * LANES : (j + 1) * LANES]
                send_buf[b * block + j * stride : b * block + (j + 1) * stride, :] = piece
            tail = jnp.where(row == 0, ids[b : b + 1], jnp.where(row == 1, ids[owners + b : owners + b + 1], 0.0))
            send_buf[(b + 1) * block - 8 : (b + 1) * block, :] = tail.astype(BF16)
        at = slice(k * part * block, (k + 1) * part * block)
        copies.append(pltpu.make_async_copy(send_buf.at[at, :], send_ref.at[at, :], sems.at[2 + k]))
        copies[k].start()
    for c in copies:
        c.wait()


def split_kernel(keep, self_ref, neg_ref, old_ref, bank_ref, neg_col_ref, old_col_ref, held_ref, parts_ref, spread_ref, bank_buf, sem):
    owned, width = bank_buf.shape
    negs = neg_ref.shape[1]
    load = pltpu.make_async_copy(bank_ref, bank_buf, sem)
    load.start()
    me = self_ref[0]
    wanted = neg_ref[pl.ds(me, 1), :] - me * owned
    wanted = jnp.concatenate([wanted] * (LANES // negs), axis=1)
    neg_col = id_col(wanted)[0:negs, :]
    neg_col_ref[...] = jnp.broadcast_to(neg_col, neg_col_ref.shape)
    same = neg_col == iota((negs, owned), 1)
    old = jnp.sum(jnp.where(same, old_ref[...], 0.0), axis=1, keepdims=True)
    old_col_ref[...] = jnp.broadcast_to(old, old_col_ref.shape)
    pick = onehot(same)
    place = iota(spread_ref.shape, 1).astype(F32)
    within = place - keep * jnp.floor((place + 0.5) * (1.0 / keep))
    spread_ref[...] = onehot(within == iota(spread_ref.shape, 0).astype(F32))
    load.wait()
    bank = bank_buf[...]
    high = bank.astype(BF16)
    rest = bank - high.astype(F32)
    middle = rest.astype(BF16)
    low = (rest - middle.astype(F32)).astype(BF16)
    parts_ref[:, 0:width] = high
    parts_ref[:, width : 2 * width] = middle
    held_ref[...] = nn(pick, high) + nn(pick, middle) + nn(pick, low)


def blend(bank, sums, counts):
    safe = jnp.maximum(counts, 1.0)
    return jnp.where(counts > 0, 0.5 * bank + 0.5 * sums / safe, bank)


def mean_kernel(
    owners, after_ref, neg_ref, held_ref, parts_ref, spread_ref, got_ref,
    ids_ref, new_ref, pack_ref, rows_ref, count_ref, neg_count_ref, table,
):
    owned = parts_ref.shape[0]
    negs, width = held_ref.shape
    slots = new_ref.shape[0]
    keep = slots // owners
    block = got_ref.shape[0] // owners
    for b in range(owners):
        sent = got_ref[(b + 1) * block - 8 : (b + 1) * block, :].astype(F32)
        table[b : b + 1, :] = sent[0:1]
        table[owners + b : owners + b + 1, :] = sent[1:2]
        for j in range(width // LANES):
            at = b * block + j * keep
            rows_ref[b * keep : (b + 1) * keep, j * LANES : (j + 1) * LANES] = got_ref[at : at + keep, :]
    rows_ref[:, width:] = jnp.ones((slots, LANES), BF16)
    wide = nn(table[...].astype(BF16), spread_ref[...])
    wide = 32.0 * wide[0:owners] + wide[owners:]
    first = iota((owners, slots), 0) * keep
    spot = iota((owners, slots), 1)
    ids = jnp.sum(jnp.where((spot >= first) & (spot < first + keep), wide, 0.0), axis=0, keepdims=True)
    ids = jnp.where(ids > 0.5, ids - 1.0, float(owned)).astype(I32)
    ids_ref[...] = ids
    got = rows_ref[...]
    col = id_col(ids)
    block = 256 if slots % 256 == 0 else slots
    squares = []
    for k in range(slots // block):
        at = slice(k * block, (k + 1) * block)
        picked = nn(onehot(iota((block, owned), 1) == col[at]), parts_ref[...])
        sums = nn(onehot(col[at] == ids), got)
        count_ref[at, :] = sums[:, width:]
        new = blend(picked[:, 0:width] + picked[:, width:], sums[:, 0:width], sums[:, width : width + 1])
        new_ref[at, :] = new
        differ = got[at, 0:width].astype(F32) - new
        squares.append(jnp.sum(differ * differ, axis=1, keepdims=True))
    squared = to_row(jnp.concatenate(squares, axis=0))
    sums = nn(onehot(neg_ref[:, 0:1] == ids), got)
    neg_count_ref[...] = sums[:, width:]
    pack_ref[0:negs, :] = blend(held_ref[...], sums[:, 0:width], sums[:, width : width + 1])
    for k in range(-(-slots // width)):
        piece = squared[:, k * width : min((k + 1) * width, slots)]
        pack_ref[negs + k : negs + k + 1, 0 : piece.shape[1]] = piece


def weight_of(counts):
    safe = jnp.maximum(counts, 1.0)
    return safe * jnp.log(safe + 10.0)


def prepare_kernel(owners, owned, capacity, count_ref, label_ref, query_ref, weight_ref, slot_ref, copy_ref):
    weight_ref[...] = weight_of(count_ref[...])
    slot = slot_of(*ranks_of(label_ref[...], owners, owned, ahead(label_ref.shape[1])), capacity)
    slot_ref[...] = to_col(slot.astype(F32)).astype(I32)
    copy_ref[...] = query_ref[...]


def scale_kernel(
    capacity, self_ref, ids_ref, neg_ref, count_ref, old_ref, pack_ref, new_ref, weight_ref, other_ref,
    full_ref, own_ref, dist_ref, out_ref, full_buf, own_buf, buf, sems,
):
    slots, width = new_ref.shape
    negs = neg_ref.shape[0]
    half = negs // 2
    ids = ids_ref[...]
    pieces = []
    for k in range(-(-slots // width)):
        part = pack_ref[negs + k : negs + k + 1, :] + other_ref[negs + k : negs + k + 1, :]
        pieces.append(part[:, 0 : min(width, slots - k * width)])
    dist = jnp.sqrt(jnp.concatenate(pieces, axis=1) + 0.25)
    dist_ref[...] = dist
    total = jnp.sum(jnp.where(neg_ref[:, 0:1] == ids, dist, 0.0), axis=1, keepdims=True)
    counts = count_ref[:, 0:1]
    conc = jnp.where(counts > 0, total / weight_of(counts), old_ref[:, 0:1])
    mine = (pack_ref[0:negs, :] / conc).astype(BF16)
    other = (other_ref[0:negs, :] / conc).astype(BF16)
    full_buf[:, 0:width] = mine
    full_buf[:, width:] = other
    first = self_ref[1] == 0
    own_buf[:, 0:width] = jnp.where(first, mine[0:half], mine[half:])
    own_buf[:, width:] = jnp.where(first, other[0:half], other[half:])
    copies = [pltpu.make_async_copy(full_buf, full_ref, sems.at[0]), pltpu.make_async_copy(own_buf, own_ref, sems.at[1])]
    for c in copies:
        c.start()
    owners = out_ref.shape[0] // capacity
    stride = slots // owners
    col = id_col(ids)
    parts = 2
    for k in range(parts):
        at = slice(k * slots // parts, (k + 1) * slots // parts)
        total = jnp.sum(jnp.where(col[at] == ids, dist, 0.0), axis=1, keepdims=True)
        scaled = new_ref[at, :] / (total / weight_ref[at, 0:1])
        few = owners // parts
        to = slice(k * few * capacity, (k + 1) * few * capacity)
        if stride == capacity:
            buf[to, :] = scaled.astype(BF16)
        for b in range(few if stride != capacity else 0):
            at = (k * few + b) * capacity
            buf[at : at + capacity, :] = scaled[b * stride : b * stride + capacity].astype(BF16)
        copies.append(pltpu.make_async_copy(buf.at[to, :], out_ref.at[to, :], sems.at[2 + k]))
        copies[-1].start()
    for c in copies:
        c.wait()


def join_kernel(*refs):
    pieces, joined = refs[:-1], refs[-1]
    at = 0
    for p in pieces:
        joined[at : at + p.shape[0], :] = p[...]
        at += p.shape[0]


def again_kernel(after_ref, value_ref, out_ref):
    out_ref[...] = value_ref[...]


def owner_kernel(ids_ref, dist_ref, got_ref, bank_ref, old_ref, new_ref, conc_ref):
    block = bank_ref.shape[0]
    slots = got_ref.shape[0]
    base = pl.program_id(0) * block
    same = jnp.where(iota((block, slots), 0) + base == ids_ref[...], 1.0, 0.0)
    width = bank_ref.shape[1]
    sums = nn(same.astype(BF16), got_ref[...])
    new_ref[...] = blend(bank_ref[...], sums[:, 0:width], sums[:, width : width + 1])
    turned = iota((slots, block), 1) + base == id_col(ids_ref[...])
    counts = jnp.sum(jnp.where(turned, 1.0, 0.0), axis=0, keepdims=True)
    total = jnp.sum(jnp.where(turned, to_col(dist_ref[...])[:, 0:1], 0.0), axis=0, keepdims=True)
    conc_ref[...] = jnp.where(counts > 0, total / weight_of(counts), old_ref[...])


def owner_call(ids, dist, got, bank, old):
    owned, width = bank.shape
    slots = got.shape[0]
    block = 256
    whole = lambda k: (0, 0)
    return pl.pallas_call(
        owner_kernel,
        grid=(owned // block,),
        in_specs=[
            pl.BlockSpec((1, slots), whole),
            pl.BlockSpec((1, slots), whole),
            pl.BlockSpec(got.shape, whole),
            pl.BlockSpec((block, width), lambda k: (k, 0)),
            pl.BlockSpec((1, block), lambda k: (0, k)),
        ],
        out_specs=[pl.BlockSpec((block, width), lambda k: (k, 0)), pl.BlockSpec((1, block), lambda k: (0, k))],
        out_shape=[shape((owned, width), F32), shape((1, owned), F32)],
        name="owner_kernel",
        compiler_params=pltpu.CompilerParams(vmem_limit_bytes=VMEM),
        cost_estimate=pl.CostEstimate(flops=20000000000, bytes_accessed=8 * owned * width, transcendentals=0),
    )(ids, dist, got, placed(bank, pltpu.HBM), placed(old, pltpu.HBM))


def logits_kernel(after_ref, mine_ref, other_ref, *refs):
    parts, (weight_ref, negs_ref, stats_ref) = refs[:-3], refs[-3:]
    rows, width = mine_ref.shape
    at = 0
    for p in parts:
        negs_ref[at : at + p.shape[0], :] = p[...]
        at += p.shape[0]
    logits = nt(mine_ref[...], negs_ref[:, 0:width]) + nt(other_ref[...], negs_ref[:, width:])
    top = jnp.max(logits, axis=1, keepdims=True)
    weight = jnp.exp(logits - top)
    weight_ref[...] = weight.astype(BF16)
    total = jnp.sum(weight, axis=1, keepdims=True)
    lane = iota((rows, LANES), 1)
    stats = jnp.transpose(jnp.where(lane == 0, top, jnp.where(lane == 1, total, 0.0)))
    stats_ref[...] = stats[0:8, :]


def pull_kernel(weight_ref, negs_ref, keep_ref, send_ref):
    width = keep_ref.shape[1]
    grad = nn(weight_ref[...], negs_ref[...])
    send_ref[...] = grad[:, width:]
    keep_ref[...] = grad[:, 0:width]


def positive_kernel(slot_ref, query_ref, back_ref, rows_ref, part_ref):
    rows, slots = query_ref.shape[0], back_ref.shape[0]
    found = nn(onehot(iota((rows, slots), 1) == slot_ref[:, 0:1]), back_ref[...])
    rows_ref[...] = found.astype(BF16)
    part = to_row(jnp.sum(query_ref[...].astype(F32) * found, axis=1, keepdims=True))
    part_ref[...] = jnp.broadcast_to(part, part_ref.shape)


def factor_kernel(self_ref, part_ref, far_ref, here_ref, there_ref, loss_ref, factor_ref):
    rows = part_ref.shape[1]
    first = self_ref[1] == 0
    here, there = here_ref[0:2, :], there_ref[0:2, :]
    low = jnp.where(first, here, there)
    high = jnp.where(first, there, here)
    positive = part_ref[0:1, :] + far_ref[0:1, :]
    top = jnp.maximum(jnp.maximum(low[0:1], high[0:1]), positive)
    exppos = jnp.exp(positive - top)
    total = low[1:2] * jnp.exp(low[0:1] - top) + high[1:2] * jnp.exp(high[0:1] - top) + exppos
    loss_ref[...] = jnp.log(total) + top - positive
    factors = jnp.concatenate(
        [jnp.exp(here[0:1] - top) / total, jnp.exp(there[0:1] - top) / total, exppos / total - 1.0], axis=0
    )
    factor_ref[...] = jnp.transpose(jnp.concatenate([factors, jnp.zeros((LANES - 3, rows), F32)], axis=0))


def final_kernel(factor_ref, rows_ref, keep_ref, sent_ref, lost_ref, grad_ref, loss_ref, grad_buf, sems):
    rows = keep_ref.shape[0]
    half = rows // 2
    copies = [pltpu.make_async_copy(lost_ref, loss_ref, sems.at[2])]
    copies[0].start()
    for k in range(2):
        at = slice(k * half, (k + 1) * half)
        mine, other, pull = (factor_ref[at, j : j + 1] for j in range(3))
        grad_buf[at, :] = keep_ref[at, :] * mine + sent_ref[at, :] * other + pull * rows_ref[at, :].astype(F32)
        copies.append(pltpu.make_async_copy(grad_buf.at[at, :], grad_ref.at[at, :], sems.at[k]))
        copies[-1].start()
    for c in copies:
        c.wait()


def swap(value):
    return lax.ppermute(value, "mp", [(0, 1), (1, 0)])


def hop(value, count, bits):
    return lax.ppermute(value, "dp", [(k, k ^ bits) for k in range(count)])


def two_hop(value, count, bits):
    return lax.ppermute(
        value, ("dp", "mp"), [(2 * k + c, 2 * (k ^ bits[c]) + c) for k in range(count) for c in range(2)]
    )


def body(features, labels, queries, bank, old_conc, neg_index):
    count = lax.axis_size("dp")
    me, core = lax.axis_index("dp"), lax.axis_index("mp")
    owned, width = bank.shape
    rows = features.shape[0]
    capacity = 3 * rows // count
    stride = 8 * -(-capacity // 8)
    block = stride * (width // LANES) + 8
    slots = count * stride
    negs = neg_index.shape[0] // count
    half = negs // 2
    place = jnp.stack([me, core]).astype(I32)
    loads = [pltpu.VMEM((1, rows), I32), pltpu.VMEM((rows, width), BF16)]

    label_row = labels.reshape(1, rows)
    (send,) = call(
        functools.partial(pack_kernel, count, owned, stride),
        (shape((count * block, LANES), BF16),),
        label_row, features, flops=2 * slots * rows * width, hbm=(0, 1), out_hbm=(0,),
        scratch=[*loads, pltpu.VMEM((count * block, LANES), BF16), pltpu.SemaphoreType.DMA((6,))],
    )
    query_far = swap(queries)
    got = lax.all_to_all(send.reshape(count, block, LANES), "dp", split_axis=0, concat_axis=0)
    got = got.reshape(count * block, LANES)

    neg_col, old_col, held, parts, spread = call(
        functools.partial(split_kernel, stride),
        (
            shape((negs, LANES), I32), shape((negs, LANES), F32), shape((negs, width), F32),
            shape((owned, 2 * width), BF16), shape((LANES, slots), BF16),
        ),
        place, neg_index.reshape(count, negs), old_conc.reshape(1, owned), bank, smem=(0,), hbm=(3,), free=(1, 2),
        scratch=[pltpu.VMEM((owned, width), F32), pltpu.SemaphoreType.DMA],
    )
    extra = 8 * -(-slots // (8 * width))
    ids, new, pack, got, counts, neg_counts = call(
        functools.partial(mean_kernel, count),
        (
            shape((1, slots), I32), shape((slots, width), F32), shape((negs + extra, width), F32),
            shape((slots, width + LANES), BF16), shape((slots, LANES), F32), shape((negs, LANES), F32),
        ),
        query_far, neg_col, held, parts, spread, got, flops=8 * slots * owned * width, hbm=(0,),
        scratch=[pltpu.VMEM((2 * count, LANES), F32)],
    )
    weights, slot, query = call(
        functools.partial(prepare_kernel, count, owned, capacity),
        (shape((slots, LANES), F32), shape((rows, LANES), I32), shape((rows, width), BF16)),
        counts, label_row, queries, free=(1, 2),
    )
    full, own, dist, scaled = call(
        functools.partial(scale_kernel, capacity),
        (
            shape((negs, 2 * width), BF16), shape((half, 2 * width), BF16), shape((1, slots), F32),
            shape((count * capacity, width), BF16),
        ),
        place, ids, neg_col, neg_counts, old_col, pack, new, weights, swap(pack), smem=(0,), out_hbm=(0, 1, 3),
        scratch=[
            pltpu.VMEM((negs, 2 * width), BF16), pltpu.VMEM((half, 2 * width), BF16),
            pltpu.VMEM((count * capacity, width), BF16), pltpu.SemaphoreType.DMA((4,)),
        ],
    )
    step = count // 4
    line = [own, two_hop(full, count, (step, 2 * step)), hop(own, count, 3 * step)]
    (joined,) = call(join_kernel, (shape((sum(p.shape[0] for p in line), 2 * width), BF16),), *line)
    back = lax.all_to_all(scaled.reshape(count, capacity, width), "dp", split_axis=0, concat_axis=0)
    new_bank, new_conc = owner_call(ids, dist, got, bank, old_conc.reshape(1, owned))
    if step == 4:
        first = two_hop(joined, count, (1, 2))
        second = two_hop(joined, count, (2, 1))
        (again,) = call(again_kernel, (shape(joined.shape, BF16),), new_conc, first, hbm=(0,))
        pieces = [joined, again, second, two_hop(again, count, (2, 1))]
    while step > 1 and step != 4:
        few = min(4, step)
        step //= few
        pieces = [joined] + [hop(joined, count, step * k) for k in range(1, few)]
        if step > 1:
            joined = jnp.concatenate(pieces, axis=0)
    found, part = call(
        positive_kernel,
        (shape((rows, width), BF16), shape((8, rows), F32)),
        slot, query, back.reshape(count * capacity, width), flops=2 * slots * rows * width,
    )
    weight, all_negs, stats = call(
        logits_kernel,
        (shape((rows, half * count), BF16), shape((half * count, 2 * width), BF16), shape((8, rows), F32)),
        part, query, query_far, *pieces, flops=4 * rows * half * count * width, free=range(2, 99),
    )
    far_stats = swap(stats)
    keep, sent = call(
        pull_kernel,
        (shape((rows, width), F32), shape((rows, width), F32)),
        weight, all_negs, flops=4 * rows * half * count * width,
    )
    sent = swap(sent)
    loss, factors = call(
        factor_kernel,
        (shape((1, rows), F32), shape((rows, LANES), F32)),
        place, part, swap(part), stats, far_stats, smem=(0,),
    )
    grad, loss = call(
        final_kernel,
        (shape((rows, width), F32), shape((1, rows), F32)),
        factors, found, keep, sent, loss, out_hbm=(0, 1),
        scratch=[pltpu.VMEM((rows, width), F32), pltpu.SemaphoreType.DMA((3,))],
    )
    return (new_bank, new_conc.reshape(owned), loss.reshape(rows), grad)


def solution(mesh):
    placed = (P("dp", "mp"), P("dp"), P("dp", "mp"), P("dp", "mp"), P("dp"), P())
    return jax.shard_map(
        body,
        mesh=mesh,
        in_specs=placed,
        out_specs=(P("dp", "mp"), P("dp"), P("dp"), P("dp", "mp")),
        check_vma=False,
    )
```

```python
import functools

import jax
import jax.numpy as jnp
from jax import lax
from jax.experimental import pallas as pl
from jax.experimental.pallas import tpu as pltpu
from jax.sharding import PartitionSpec as P

F32 = jnp.float32
BF16 = jnp.bfloat16
I32 = jnp.int32
LANES = 128
VMEM = 24 * 2**20
OUT = (7, 14, 5, 13, 8, 10, 15, 11, 0, 3, 9, 1, 2, 12, 6, 4)
BACK = (4, 0, 5, 6, 8, 12, 2, 3, 1, 11, 9, 14, 15, 10, 13, 7)


def call(kernel, outs, *args, flops=0, smem=(), hbm=(), out_hbm=(), free=(), out_free=(), scratch=()):
    moved = sum(a.size * a.dtype.itemsize for a in args) + sum(o.size * o.dtype.itemsize for o in outs)
    spaces = [pltpu.SMEM if k in smem else pltpu.HBM if k in hbm else pltpu.VMEM for k in range(len(args))]
    out_spaces = [pltpu.HBM if k in out_hbm else pltpu.VMEM for k in range(len(outs))]
    return pl.pallas_call(
        kernel,
        out_shape=[o if k in out_free else space(o.shape, o.dtype) for k, (o, space) in enumerate(zip(outs, out_spaces))],
        in_specs=[pl.BlockSpec(memory_space=space) for space in spaces],
        out_specs=[pl.BlockSpec(memory_space=space) for space in out_spaces],
        scratch_shapes=list(scratch),
        name=getattr(kernel, "func", kernel).__name__,
        compiler_params=pltpu.CompilerParams(vmem_limit_bytes=VMEM),
        cost_estimate=pl.CostEstimate(flops=flops, bytes_accessed=moved, transcendentals=0),
    )(*[placed(a, space, k in free) for k, (a, space) in enumerate(zip(args, spaces))])


def placed(value, space, free=False):
    return value if free or space is pltpu.SMEM else pltpu.with_memory_space_constraint(value, space)


def shape(dims, dtype):
    return jax.ShapeDtypeStruct(dims, dtype)


def nt(a, b):
    return lax.dot_general(a, b, (((1,), (1,)), ((), ())), preferred_element_type=F32)


def nn(a, b):
    return jnp.dot(a, b, preferred_element_type=F32)


def iota(dims, axis):
    return lax.broadcasted_iota(I32, dims, axis)


def onehot(mask):
    return jnp.where(mask, 1.0, 0.0).astype(BF16)


def to_col(row):
    return jnp.transpose(jnp.broadcast_to(row, (LANES, row.shape[1])))


def to_row(col):
    return jnp.transpose(jnp.broadcast_to(col, (col.shape[0], LANES)))[0:1, :]


def id_col(ids):
    return to_col(ids.astype(F32))[:, 0:1].astype(I32)


def ahead(rows):
    return onehot(iota((rows, rows), 0) <= iota((rows, rows), 1))


def ranks_of(label, owners, owned, before):
    start = iota((owners, label.shape[1]), 0) * owned
    mine = (label >= start) & (label < start + owned)
    running = nn(onehot(mine), before)
    return mine, jnp.sum(jnp.where(mine, running, 0.0), axis=0, keepdims=True) - 1.0


def order_of(owners, order):
    return order if owners == len(order) else tuple(range(owners))


def slot_of(mine, rank, stride, order):
    owners = mine.shape[0]
    owner = place = iota(mine.shape, 0)
    for k, device in enumerate(order_of(owners, order)):
        place = jnp.where(owner == device, k, place) if k != device else place
    place = jnp.sum(jnp.where(mine, place.astype(F32), 0.0), axis=0, keepdims=True)
    return (place * stride + rank).astype(I32)


def exchange(value, order):
    groups = [list(order_of(lax.axis_size("dp"), order))]
    return lax.all_to_all(value, "dp", split_axis=0, concat_axis=0, axis_index_groups=groups)


def pack_kernel(owners, owned, stride, label_ref, feat_ref, send_ref, label_buf, feat_buf, send_buf, sems):
    rows, width = feat_buf.shape
    block = send_buf.shape[0] // owners
    labels = pltpu.make_async_copy(label_ref, label_buf, sems.at[0])
    feats = pltpu.make_async_copy(feat_ref, feat_buf, sems.at[1])
    labels.start()
    feats.start()
    before = ahead(rows)
    labels.wait()
    label = label_buf[...]
    mine, rank = ranks_of(label, owners, owned, before)
    slot = slot_of(mine, rank, stride, OUT)
    value = jnp.where(mine, (label - iota((owners, rows), 0) * owned + 1).astype(F32), 0.0)
    high = jnp.floor(value * (1.0 / 32.0))
    value = jnp.concatenate([high, value - 32.0 * high], axis=0).astype(BF16)
    ids = nt(value, onehot(iota((LANES, rows), 0).astype(F32) == rank))
    feats.wait()
    chunks = 4
    part = owners // chunks
    copies = []
    row = iota((8, LANES), 0)
    for k in range(chunks):
        spot = iota((part * stride, rows), 0) + k * part * stride
        picked = nn(onehot(spot == slot), feat_buf[...]).astype(BF16)
        for c in range(part):
            b = k * part + c
            for j in range(width // LANES):
                piece = picked[c * stride : (c + 1) * stride, j * LANES : (j + 1) * LANES]
                send_buf[b * block + j * stride : b * block + (j + 1) * stride, :] = piece
            o = order_of(owners, OUT)[b]
            tail = jnp.where(row == 0, ids[o : o + 1], jnp.where(row == 1, ids[owners + o : owners + o + 1], 0.0))
            send_buf[(b + 1) * block - 8 : (b + 1) * block, :] = tail.astype(BF16)
        at = slice(k * part * block, (k + 1) * part * block)
        copies.append(pltpu.make_async_copy(send_buf.at[at, :], send_ref.at[at, :], sems.at[2 + k]))
        copies[k].start()
    for c in copies:
        c.wait()


def split_kernel(keep, self_ref, neg_ref, old_ref, bank_ref, neg_col_ref, old_col_ref, held_ref, parts_ref, spread_ref, bank_buf, sem):
    owned, width = bank_buf.shape
    negs = neg_ref.shape[1]
    load = pltpu.make_async_copy(bank_ref, bank_buf, sem)
    load.start()
    me = self_ref[0]
    wanted = neg_ref[pl.ds(me, 1), :] - me * owned
    wanted = jnp.concatenate([wanted] * (LANES // negs), axis=1)
    neg_col = id_col(wanted)[0:negs, :]
    neg_col_ref[...] = jnp.broadcast_to(neg_col, neg_col_ref.shape)
    same = neg_col == iota((negs, owned), 1)
    old = jnp.sum(jnp.where(same, old_ref[...], 0.0), axis=1, keepdims=True)
    old_col_ref[...] = jnp.broadcast_to(old, old_col_ref.shape)
    pick = onehot(same)
    place = iota(spread_ref.shape, 1).astype(F32)
    within = place - keep * jnp.floor((place + 0.5) * (1.0 / keep))
    spread_ref[...] = onehot(within == iota(spread_ref.shape, 0).astype(F32))
    load.wait()
    bank = bank_buf[...]
    high = bank.astype(BF16)
    rest = bank - high.astype(F32)
    middle = rest.astype(BF16)
    low = (rest - middle.astype(F32)).astype(BF16)
    parts_ref[:, 0:width] = high
    parts_ref[:, width : 2 * width] = middle
    held_ref[...] = nn(pick, high) + nn(pick, middle) + nn(pick, low)


def blend(bank, sums, counts):
    safe = jnp.maximum(counts, 1.0)
    return jnp.where(counts > 0, 0.5 * bank + 0.5 * sums / safe, bank)


def mean_kernel(
    owners, after_ref, neg_ref, held_ref, parts_ref, spread_ref, got_ref,
    ids_ref, new_ref, pack_ref, rows_ref, count_ref, neg_count_ref, table,
):
    owned = parts_ref.shape[0]
    negs, width = held_ref.shape
    slots = new_ref.shape[0]
    keep = slots // owners
    block = got_ref.shape[0] // owners
    for b in range(owners):
        c = order_of(owners, OUT).index(order_of(owners, BACK)[b])
        sent = got_ref[(c + 1) * block - 8 : (c + 1) * block, :].astype(F32)
        table[b : b + 1, :] = sent[0:1]
        table[owners + b : owners + b + 1, :] = sent[1:2]
        for j in range(width // LANES):
            at = c * block + j * keep
            rows_ref[b * keep : (b + 1) * keep, j * LANES : (j + 1) * LANES] = got_ref[at : at + keep, :]
    rows_ref[:, width:] = jnp.ones((slots, LANES), BF16)
    wide = nn(table[...].astype(BF16), spread_ref[...])
    wide = 32.0 * wide[0:owners] + wide[owners:]
    first = iota((owners, slots), 0) * keep
    spot = iota((owners, slots), 1)
    ids = jnp.sum(jnp.where((spot >= first) & (spot < first + keep), wide, 0.0), axis=0, keepdims=True)
    ids = jnp.where(ids > 0.5, ids - 1.0, float(owned)).astype(I32)
    ids_ref[...] = ids
    got = rows_ref[...]
    col = id_col(ids)
    block = 256 if slots % 256 == 0 else slots
    squares = []
    for k in range(slots // block):
        at = slice(k * block, (k + 1) * block)
        picked = nn(onehot(iota((block, owned), 1) == col[at]), parts_ref[...])
        sums = nn(onehot(col[at] == ids), got)
        count_ref[at, :] = sums[:, width:]
        new = blend(picked[:, 0:width] + picked[:, width:], sums[:, 0:width], sums[:, width : width + 1])
        new_ref[at, :] = new
        differ = got[at, 0:width].astype(F32) - new
        squares.append(jnp.sum(differ * differ, axis=1, keepdims=True))
    squared = to_row(jnp.concatenate(squares, axis=0))
    sums = nn(onehot(neg_ref[:, 0:1] == ids), got)
    neg_count_ref[...] = sums[:, width:]
    pack_ref[0:negs, :] = blend(held_ref[...], sums[:, 0:width], sums[:, width : width + 1])
    for k in range(-(-slots // width)):
        piece = squared[:, k * width : min((k + 1) * width, slots)]
        pack_ref[negs + k : negs + k + 1, 0 : piece.shape[1]] = piece


def weight_of(counts):
    safe = jnp.maximum(counts, 1.0)
    return safe * jnp.log(safe + 10.0)


def prepare_kernel(owners, owned, capacity, count_ref, label_ref, query_ref, weight_ref, slot_ref, copy_ref):
    weight_ref[...] = weight_of(count_ref[...])
    slot = slot_of(*ranks_of(label_ref[...], owners, owned, ahead(label_ref.shape[1])), capacity, BACK)
    slot_ref[...] = to_col(slot.astype(F32)).astype(I32)
    copy_ref[...] = query_ref[...]


def scale_kernel(
    capacity, self_ref, ids_ref, neg_ref, count_ref, old_ref, pack_ref, new_ref, weight_ref, other_ref,
    full_ref, own_ref, dist_ref, out_ref, own_buf, full_buf, buf, sems,
):
    slots, width = new_ref.shape
    negs = neg_ref.shape[0]
    half = negs // 2
    ids = ids_ref[...]
    pieces = []
    for k in range(-(-slots // width)):
        part = pack_ref[negs + k : negs + k + 1, :] + other_ref[negs + k : negs + k + 1, :]
        pieces.append(part[:, 0 : min(width, slots - k * width)])
    dist = jnp.sqrt(jnp.concatenate(pieces, axis=1) + 0.25)
    dist_ref[...] = dist
    total = jnp.sum(jnp.where(neg_ref[:, 0:1] == ids, dist, 0.0), axis=1, keepdims=True)
    counts = count_ref[:, 0:1]
    conc = jnp.where(counts > 0, total / weight_of(counts), old_ref[:, 0:1])
    mine = (pack_ref[0:negs, :] / conc).astype(BF16)
    other = (other_ref[0:negs, :] / conc).astype(BF16)
    full_buf[:, 0:width] = mine
    full_buf[:, width:] = other
    first = self_ref[1] == 0
    own_buf[:, 0:width] = jnp.where(first, mine[0:half], mine[half:])
    own_buf[:, width:] = jnp.where(first, other[0:half], other[half:])
    copies = [pltpu.make_async_copy(full_buf, full_ref, sems.at[0]), pltpu.make_async_copy(own_buf, own_ref, sems.at[1])]
    for c in copies:
        c.start()
    owners = out_ref.shape[0] // capacity
    stride = slots // owners
    col = id_col(ids)
    parts = 2
    for k in range(parts):
        at = slice(k * slots // parts, (k + 1) * slots // parts)
        total = jnp.sum(jnp.where(col[at] == ids, dist, 0.0), axis=1, keepdims=True)
        scaled = new_ref[at, :] / (total / weight_ref[at, 0:1])
        few = owners // parts
        to = slice(k * few * capacity, (k + 1) * few * capacity)
        if stride == capacity:
            buf[to, :] = scaled.astype(BF16)
        for b in range(few if stride != capacity else 0):
            at = (k * few + b) * capacity
            buf[at : at + capacity, :] = scaled[b * stride : b * stride + capacity].astype(BF16)
        copies.append(pltpu.make_async_copy(buf.at[to, :], out_ref.at[to, :], sems.at[2 + k]))
        copies[-1].start()
    for c in copies:
        c.wait()


def join_kernel(*refs):
    pieces, joined = refs[:-1], refs[-1]
    at = 0
    for p in pieces:
        joined[at : at + p.shape[0], :] = p[...]
        at += p.shape[0]


def again_kernel(after_ref, value_ref, out_ref):
    out_ref[...] = value_ref[...]


def owner_kernel(ids_ref, dist_ref, got_ref, bank_ref, old_ref, new_ref, conc_ref):
    block = bank_ref.shape[0]
    slots = got_ref.shape[0]
    base = pl.program_id(0) * block
    same = jnp.where(iota((block, slots), 0) + base == ids_ref[...], 1.0, 0.0)
    width = bank_ref.shape[1]
    sums = nn(same.astype(BF16), got_ref[...])
    new_ref[...] = blend(bank_ref[...], sums[:, 0:width], sums[:, width : width + 1])
    turned = iota((slots, block), 1) + base == id_col(ids_ref[...])
    counts = jnp.sum(jnp.where(turned, 1.0, 0.0), axis=0, keepdims=True)
    total = jnp.sum(jnp.where(turned, to_col(dist_ref[...])[:, 0:1], 0.0), axis=0, keepdims=True)
    conc_ref[...] = jnp.where(counts > 0, total / weight_of(counts), old_ref[...])


def owner_call(ids, dist, got, bank, old):
    owned, width = bank.shape
    slots = got.shape[0]
    block = 256
    whole = lambda k: (0, 0)
    return pl.pallas_call(
        owner_kernel,
        grid=(owned // block,),
        in_specs=[
            pl.BlockSpec((1, slots), whole),
            pl.BlockSpec((1, slots), whole),
            pl.BlockSpec(got.shape, whole),
            pl.BlockSpec((block, width), lambda k: (k, 0)),
            pl.BlockSpec((1, block), lambda k: (0, k)),
        ],
        out_specs=[pl.BlockSpec((block, width), lambda k: (k, 0)), pl.BlockSpec((1, block), lambda k: (0, k))],
        out_shape=[shape((owned, width), F32), shape((1, owned), F32)],
        name="owner_kernel",
        compiler_params=pltpu.CompilerParams(vmem_limit_bytes=VMEM),
        cost_estimate=pl.CostEstimate(flops=20000000000, bytes_accessed=8 * owned * width, transcendentals=0),
    )(ids, dist, got, placed(bank, pltpu.HBM), placed(old, pltpu.HBM))


def logits_kernel(after_ref, mine_ref, other_ref, *refs):
    parts, (weight_ref, negs_ref, stats_ref) = refs[:-3], refs[-3:]
    rows, width = mine_ref.shape
    at = 0
    for p in parts:
        negs_ref[at : at + p.shape[0], :] = p[...]
        at += p.shape[0]
    logits = nt(mine_ref[...], negs_ref[:, 0:width]) + nt(other_ref[...], negs_ref[:, width:])
    top = jnp.max(logits, axis=1, keepdims=True)
    weight = jnp.exp(logits - top)
    weight_ref[...] = weight.astype(BF16)
    total = jnp.sum(weight, axis=1, keepdims=True)
    lane = iota((rows, LANES), 1)
    stats = jnp.transpose(jnp.where(lane == 0, top, jnp.where(lane == 1, total, 0.0)))
    stats_ref[...] = stats[0:8, :]


def pull_kernel(weight_ref, negs_ref, far_ref):
    far_ref[...] = nn(weight_ref[...], negs_ref[:, far_ref.shape[1] :])


def near_kernel(after_ref, weight_ref, negs_ref, near_ref):
    near_ref[...] = nn(weight_ref[...], negs_ref[:, 0 : near_ref.shape[1]])


def positive_kernel(slot_ref, query_ref, back_ref, rows_ref, part_ref):
    rows, slots = query_ref.shape[0], back_ref.shape[0]
    found = nn(onehot(iota((rows, slots), 1) == slot_ref[:, 0:1]), back_ref[...])
    rows_ref[...] = found.astype(BF16)
    part = to_row(jnp.sum(query_ref[...].astype(F32) * found, axis=1, keepdims=True))
    part_ref[...] = jnp.broadcast_to(part, part_ref.shape)


def factor_kernel(self_ref, part_ref, far_ref, here_ref, there_ref, loss_ref, factor_ref):
    rows = part_ref.shape[1]
    first = self_ref[1] == 0
    here, there = here_ref[0:2, :], there_ref[0:2, :]
    low = jnp.where(first, here, there)
    high = jnp.where(first, there, here)
    positive = part_ref[0:1, :] + far_ref[0:1, :]
    top = jnp.maximum(jnp.maximum(low[0:1], high[0:1]), positive)
    exppos = jnp.exp(positive - top)
    total = low[1:2] * jnp.exp(low[0:1] - top) + high[1:2] * jnp.exp(high[0:1] - top) + exppos
    loss_ref[...] = jnp.log(total) + top - positive
    factors = jnp.concatenate(
        [jnp.exp(here[0:1] - top) / total, jnp.exp(there[0:1] - top) / total, exppos / total - 1.0], axis=0
    )
    factor_ref[...] = jnp.transpose(jnp.concatenate([factors, jnp.zeros((LANES - 3, rows), F32)], axis=0))


def final_kernel(factor_ref, rows_ref, keep_ref, sent_ref, lost_ref, grad_ref, loss_ref, grad_buf, sems):
    rows = keep_ref.shape[0]
    half = rows // 2
    copies = [pltpu.make_async_copy(lost_ref, loss_ref, sems.at[2])]
    copies[0].start()
    for k in range(2):
        at = slice(k * half, (k + 1) * half)
        mine, other, pull = (factor_ref[at, j : j + 1] for j in range(3))
        grad_buf[at, :] = keep_ref[at, :] * mine + sent_ref[at, :] * other + pull * rows_ref[at, :].astype(F32)
        copies.append(pltpu.make_async_copy(grad_buf.at[at, :], grad_ref.at[at, :], sems.at[k]))
        copies[-1].start()
    for c in copies:
        c.wait()


def swap(value):
    return lax.ppermute(value, "mp", [(0, 1), (1, 0)])


def hop(value, count, bits):
    return lax.ppermute(value, "dp", [(k, k ^ bits) for k in range(count)])


def two_hop(value, count, bits):
    return lax.ppermute(
        value, ("dp", "mp"), [(2 * k + c, 2 * (k ^ bits[c]) + c) for k in range(count) for c in range(2)]
    )


def body(features, labels, queries, bank, old_conc, neg_index):
    count = lax.axis_size("dp")
    me, core = lax.axis_index("dp"), lax.axis_index("mp")
    owned, width = bank.shape
    rows = features.shape[0]
    capacity = 3 * rows // count
    stride = 8 * -(-capacity // 8)
    block = stride * (width // LANES) + 8
    slots = count * stride
    negs = neg_index.shape[0] // count
    half = negs // 2
    place = jnp.stack([me, core]).astype(I32)
    loads = [pltpu.VMEM((1, rows), I32), pltpu.VMEM((rows, width), BF16)]

    label_row = labels.reshape(1, rows)
    (send,) = call(
        functools.partial(pack_kernel, count, owned, stride),
        (shape((count * block, LANES), BF16),),
        label_row, features, flops=2 * slots * rows * width, hbm=(0, 1), out_hbm=(0,),
        scratch=[*loads, pltpu.VMEM((count * block, LANES), BF16), pltpu.SemaphoreType.DMA((6,))],
    )
    query_far = swap(queries)
    got = exchange(send.reshape(count, block, LANES), OUT)
    got = got.reshape(count * block, LANES)

    neg_col, old_col, held, parts, spread = call(
        functools.partial(split_kernel, stride),
        (
            shape((negs, LANES), I32), shape((negs, LANES), F32), shape((negs, width), F32),
            shape((owned, 2 * width), BF16), shape((LANES, slots), BF16),
        ),
        place, neg_index.reshape(count, negs), old_conc.reshape(1, owned), bank, smem=(0,), hbm=(3,), free=(1, 2),
        scratch=[pltpu.VMEM((owned, width), F32), pltpu.SemaphoreType.DMA],
    )
    extra = 8 * -(-slots // (8 * width))
    ids, new, pack, got, counts, neg_counts = call(
        functools.partial(mean_kernel, count),
        (
            shape((1, slots), I32), shape((slots, width), F32), shape((negs + extra, width), F32),
            shape((slots, width + LANES), BF16), shape((slots, LANES), F32), shape((negs, LANES), F32),
        ),
        query_far, neg_col, held, parts, spread, got, flops=8 * slots * owned * width, hbm=(0,),
        scratch=[pltpu.VMEM((2 * count, LANES), F32)],
    )
    weights, slot, query = call(
        functools.partial(prepare_kernel, count, owned, capacity),
        (shape((slots, LANES), F32), shape((rows, LANES), I32), shape((rows, width), BF16)),
        counts, label_row, queries, free=(1, 2),
    )
    full, own, dist, scaled, own_near = call(
        functools.partial(scale_kernel, capacity),
        (
            shape((negs, 2 * width), BF16), shape((half, 2 * width), BF16), shape((1, slots), F32),
            shape((count * capacity, width), BF16), shape((half, 2 * width), BF16),
        ),
        place, ids, neg_col, neg_counts, old_col, pack, new, weights, swap(pack), smem=(0,), out_hbm=(0, 1, 3),
        scratch=[
            pltpu.VMEM((negs, 2 * width), BF16), pltpu.VMEM((count * capacity, width), BF16),
            pltpu.SemaphoreType.DMA((4,)),
        ],
    )
    step = count // 4
    line = [own_near, two_hop(full, count, (step, 2 * step)), hop(own, count, 3 * step)]
    (joined,) = call(join_kernel, (shape((sum(p.shape[0] for p in line), 2 * width), BF16),), *line)
    back = exchange(scaled.reshape(count, capacity, width), BACK)
    new_bank, new_conc = owner_call(ids, dist, got, bank, old_conc.reshape(1, owned))
    if step == 4:
        first = two_hop(joined, count, (1, 2))
        second = two_hop(joined, count, (2, 1))
        (again,) = call(again_kernel, (shape(joined.shape, BF16),), new_conc, first, hbm=(0,))
        pieces = [joined, again, second, two_hop(again, count, (2, 1))]
    while step > 1 and step != 4:
        few = min(4, step)
        step //= few
        pieces = [joined] + [hop(joined, count, step * k) for k in range(1, few)]
        if step > 1:
            joined = jnp.concatenate(pieces, axis=0)
    found, part = call(
        positive_kernel,
        (shape((rows, width), BF16), shape((8, rows), F32)),
        slot, query, back.reshape(count * capacity, width), flops=2 * slots * rows * width,
    )
    weight, all_negs, stats = call(
        logits_kernel,
        (shape((rows, half * count), BF16), shape((half * count, 2 * width), BF16), shape((8, rows), F32)),
        part, query, query_far, *pieces, flops=4 * rows * half * count * width, free=range(2, 99),
    )
    far_stats = swap(stats)
    flops = 2 * rows * half * count * width
    (sent,) = call(pull_kernel, (shape((rows, width), F32),), weight, all_negs, flops=flops)
    (keep,) = call(near_kernel, (shape((rows, width), F32),), sent, weight, all_negs, flops=flops)
    sent = swap(sent)
    loss, factors = call(
        factor_kernel,
        (shape((1, rows), F32), shape((rows, LANES), F32)),
        place, part, swap(part), stats, far_stats, smem=(0,),
    )
    grad, loss = call(
        final_kernel,
        (shape((rows, width), F32), shape((1, rows), F32)),
        factors, found, keep, sent, loss, out_hbm=(0, 1),
        scratch=[pltpu.VMEM((rows, width), F32), pltpu.SemaphoreType.DMA((3,))],
    )
    return (new_bank, new_conc.reshape(owned), loss.reshape(rows), grad)


def solution(mesh):
    placed = (P("dp", "mp"), P("dp"), P("dp", "mp"), P("dp", "mp"), P("dp"), P())
    return jax.shard_map(
        body,
        mesh=mesh,
        in_specs=placed,
        out_specs=(P("dp", "mp"), P("dp"), P("dp"), P("dp", "mp")),
        check_vma=False,
    )
```

```python
import functools

import jax
import jax.numpy as jnp
from jax import lax
from jax.experimental import pallas as pl
from jax.experimental.pallas import tpu as pltpu
from jax.sharding import PartitionSpec as P

F32 = jnp.float32
BF16 = jnp.bfloat16
I32 = jnp.int32
LANES = 128
VMEM = 24 * 2**20
OUT = (7, 14, 5, 13, 8, 10, 15, 11, 0, 2, 3, 1, 9, 12, 6, 4)
BACK = (4, 0, 5, 6, 8, 12, 2, 3, 1, 11, 9, 14, 15, 10, 13, 7)


def call(kernel, outs, *args, flops=0, hbm=(), out_hbm=(), free=(), out_free=(), scratch=()):
    moved = sum(a.size * a.dtype.itemsize for a in args) + sum(o.size * o.dtype.itemsize for o in outs)
    spaces = [pltpu.HBM if k in hbm else pltpu.VMEM for k in range(len(args))]
    out_spaces = [pltpu.HBM if k in out_hbm else pltpu.VMEM for k in range(len(outs))]
    return pl.pallas_call(
        kernel,
        out_shape=[o if k in out_free else space(o.shape, o.dtype) for k, (o, space) in enumerate(zip(outs, out_spaces))],
        in_specs=[pl.BlockSpec(memory_space=space) for space in spaces],
        out_specs=[pl.BlockSpec(memory_space=space) for space in out_spaces],
        scratch_shapes=list(scratch),
        name=getattr(kernel, "func", kernel).__name__,
        compiler_params=pltpu.CompilerParams(vmem_limit_bytes=VMEM),
        cost_estimate=pl.CostEstimate(flops=flops, bytes_accessed=moved, transcendentals=0),
    )(*[placed(a, space, k in free) for k, (a, space) in enumerate(zip(args, spaces))])


def placed(value, space, free=False):
    return value if free else pltpu.with_memory_space_constraint(value, space)


def shape(dims, dtype):
    return jax.ShapeDtypeStruct(dims, dtype)


def nt(a, b):
    return lax.dot_general(a, b, (((1,), (1,)), ((), ())), preferred_element_type=F32)


def nn(a, b):
    return jnp.dot(a, b, preferred_element_type=F32)


def iota(dims, axis):
    return lax.broadcasted_iota(I32, dims, axis)


def onehot(mask):
    return jnp.where(mask, 1.0, 0.0).astype(BF16)


def to_col(row):
    return jnp.transpose(jnp.broadcast_to(row, (LANES, row.shape[1])))


def to_row(col):
    return jnp.transpose(jnp.broadcast_to(col, (col.shape[0], LANES)))[0:1, :]


def id_col(ids):
    return to_col(ids.astype(F32))[:, 0:1].astype(I32)


def ahead(rows):
    return onehot(iota((rows, rows), 0) <= iota((rows, rows), 1))


def ranks_of(label, owners, owned, before):
    start = iota((owners, label.shape[1]), 0) * owned
    mine = (label >= start) & (label < start + owned)
    running = nn(onehot(mine), before)
    return mine, jnp.sum(jnp.where(mine, running, 0.0), axis=0, keepdims=True) - 1.0


def order_of(owners, order):
    return order if owners == len(order) else tuple(range(owners))


def slot_of(mine, rank, stride, order):
    owners = mine.shape[0]
    owner = place = iota(mine.shape, 0)
    for k, device in enumerate(order_of(owners, order)):
        place = jnp.where(owner == device, k, place) if k != device else place
    place = jnp.sum(jnp.where(mine, place.astype(F32), 0.0), axis=0, keepdims=True)
    return (place * stride + rank).astype(I32)


def exchange(value, order):
    groups = [list(order_of(lax.axis_size("dp"), order))]
    return lax.all_to_all(value, "dp", split_axis=0, concat_axis=0, axis_index_groups=groups)


def pack_kernel(owners, owned, stride, label_ref, feat_ref, send_ref, label_buf, feat_buf, send_buf, sems):
    rows, width = feat_buf.shape
    block = send_buf.shape[0] // owners
    labels = pltpu.make_async_copy(label_ref, label_buf, sems.at[0])
    feats = pltpu.make_async_copy(feat_ref, feat_buf, sems.at[1])
    labels.start()
    feats.start()
    before = ahead(rows)
    labels.wait()
    label = label_buf[...]
    mine, rank = ranks_of(label, owners, owned, before)
    slot = slot_of(mine, rank, stride, OUT)
    value = jnp.where(mine, (label - iota((owners, rows), 0) * owned + 1).astype(F32), 0.0)
    high = jnp.floor(value * (1.0 / 32.0))
    value = jnp.concatenate([high, value - 32.0 * high], axis=0).astype(BF16)
    ids = nt(value, onehot(iota((LANES, rows), 0).astype(F32) == rank))
    feats.wait()
    chunks = 4
    part = owners // chunks
    copies = []
    row = iota((8, LANES), 0)
    for k in range(chunks):
        spot = iota((part * stride, rows), 0) + k * part * stride
        picked = nn(onehot(spot == slot), feat_buf[...]).astype(BF16)
        for c in range(part):
            b = k * part + c
            for j in range(width // LANES):
                piece = picked[c * stride : (c + 1) * stride, j * LANES : (j + 1) * LANES]
                send_buf[b * block + j * stride : b * block + (j + 1) * stride, :] = piece
            o = order_of(owners, OUT)[b]
            tail = jnp.where(row == 0, ids[o : o + 1], jnp.where(row == 1, ids[owners + o : owners + o + 1], 0.0))
            send_buf[(b + 1) * block - 8 : (b + 1) * block, :] = tail.astype(BF16)
        at = slice(k * part * block, (k + 1) * part * block)
        copies.append(pltpu.make_async_copy(send_buf.at[at, :], send_ref.at[at, :], sems.at[2 + k]))
        copies[k].start()
    for c in copies:
        c.wait()


def split_kernel(keep, neg_ref, old_ref, bank_ref, neg_col_ref, old_col_ref, held_ref, parts_ref, spread_ref, bank_buf, sem):
    owned, width = bank_buf.shape
    negs = neg_ref.shape[1]
    load = pltpu.make_async_copy(bank_ref, bank_buf, sem)
    load.start()
    me = lax.axis_index("dp").astype(I32)
    wanted = neg_ref[pl.ds(me, 1), :] - me * owned
    wanted = jnp.concatenate([wanted] * (LANES // negs), axis=1)
    neg_col = id_col(wanted)[0:negs, :]
    neg_col_ref[...] = jnp.broadcast_to(neg_col, neg_col_ref.shape)
    same = neg_col == iota((negs, owned), 1)
    old = jnp.sum(jnp.where(same, old_ref[...], 0.0), axis=1, keepdims=True)
    old_col_ref[...] = jnp.broadcast_to(old, old_col_ref.shape)
    pick = onehot(same)
    place = iota(spread_ref.shape, 1).astype(F32)
    within = place - keep * jnp.floor((place + 0.5) * (1.0 / keep))
    spread_ref[...] = onehot(within == iota(spread_ref.shape, 0).astype(F32))
    load.wait()
    bank = bank_buf[...]
    high = bank.astype(BF16)
    rest = bank - high.astype(F32)
    middle = rest.astype(BF16)
    low = (rest - middle.astype(F32)).astype(BF16)
    parts_ref[:, 0:width] = high
    parts_ref[:, width : 2 * width] = middle
    held_ref[...] = nn(pick, high) + nn(pick, middle) + nn(pick, low)


def blend(bank, sums, counts):
    safe = jnp.maximum(counts, 1.0)
    return jnp.where(counts > 0, 0.5 * bank + 0.5 * sums / safe, bank)


def mean_kernel(
    owners, after_ref, neg_ref, held_ref, parts_ref, spread_ref, got_ref,
    ids_ref, new_ref, pack_ref, rows_ref, count_ref, neg_count_ref, table,
):
    owned = parts_ref.shape[0]
    negs, width = held_ref.shape
    slots = new_ref.shape[0]
    keep = slots // owners
    block = got_ref.shape[0] // owners
    for b in range(owners):
        c = order_of(owners, OUT).index(order_of(owners, BACK)[b])
        sent = got_ref[(c + 1) * block - 8 : (c + 1) * block, :].astype(F32)
        table[b : b + 1, :] = sent[0:1]
        table[owners + b : owners + b + 1, :] = sent[1:2]
        for j in range(width // LANES):
            at = c * block + j * keep
            rows_ref[b * keep : (b + 1) * keep, j * LANES : (j + 1) * LANES] = got_ref[at : at + keep, :]
    rows_ref[:, width:] = jnp.ones((slots, LANES), BF16)
    wide = nn(table[...].astype(BF16), spread_ref[...])
    wide = 32.0 * wide[0:owners] + wide[owners:]
    first = iota((owners, slots), 0) * keep
    spot = iota((owners, slots), 1)
    ids = jnp.sum(jnp.where((spot >= first) & (spot < first + keep), wide, 0.0), axis=0, keepdims=True)
    ids = jnp.where(ids > 0.5, ids - 1.0, float(owned)).astype(I32)
    ids_ref[...] = ids
    got = rows_ref[...]
    col = id_col(ids)
    block = 256 if slots % 256 == 0 else slots
    squares = []
    for k in range(slots // block):
        at = slice(k * block, (k + 1) * block)
        picked = nn(onehot(iota((block, owned), 1) == col[at]), parts_ref[...])
        sums = nn(onehot(col[at] == ids), got)
        count_ref[at, :] = sums[:, width:]
        new = blend(picked[:, 0:width] + picked[:, width:], sums[:, 0:width], sums[:, width : width + 1])
        new_ref[at, :] = new
        differ = got[at, 0:width].astype(F32) - new
        squares.append(jnp.sum(differ * differ, axis=1, keepdims=True))
    squared = to_row(jnp.concatenate(squares, axis=0))
    sums = nn(onehot(neg_ref[:, 0:1] == ids), got)
    neg_count_ref[...] = sums[:, width:]
    pack_ref[0:negs, :] = blend(held_ref[...], sums[:, 0:width], sums[:, width : width + 1])
    for k in range(-(-slots // width)):
        piece = squared[:, k * width : min((k + 1) * width, slots)]
        pack_ref[negs + k : negs + k + 1, 0 : piece.shape[1]] = piece


def weight_of(counts):
    safe = jnp.maximum(counts, 1.0)
    return safe * jnp.log(safe + 10.0)


def prepare_kernel(owners, owned, capacity, count_ref, label_ref, query_ref, weight_ref, slot_ref, copy_ref):
    weight_ref[...] = weight_of(count_ref[...])
    slot = slot_of(*ranks_of(label_ref[...], owners, owned, ahead(label_ref.shape[1])), capacity, BACK)
    slot_ref[...] = to_col(slot.astype(F32)).astype(I32)
    copy_ref[...] = query_ref[...]


def scale_kernel(
    capacity, ids_ref, neg_ref, count_ref, old_ref, pack_ref, new_ref, weight_ref, other_ref,
    full_ref, own_ref, dist_ref, out_ref, own_buf, full_buf, buf, sems,
):
    slots, width = new_ref.shape
    negs = neg_ref.shape[0]
    half = negs // 2
    ids = ids_ref[...]
    pieces = []
    for k in range(-(-slots // width)):
        part = pack_ref[negs + k : negs + k + 1, :] + other_ref[negs + k : negs + k + 1, :]
        pieces.append(part[:, 0 : min(width, slots - k * width)])
    dist = jnp.sqrt(jnp.concatenate(pieces, axis=1) + 0.25)
    dist_ref[...] = dist
    total = jnp.sum(jnp.where(neg_ref[:, 0:1] == ids, dist, 0.0), axis=1, keepdims=True)
    counts = count_ref[:, 0:1]
    conc = jnp.where(counts > 0, total / weight_of(counts), old_ref[:, 0:1])
    mine = (pack_ref[0:negs, :] / conc).astype(BF16)
    other = (other_ref[0:negs, :] / conc).astype(BF16)
    full_buf[:, 0:width] = mine
    full_buf[:, width:] = other
    first = lax.axis_index("mp") == 0
    own_buf[:, 0:width] = jnp.where(first, mine[0:half], mine[half:])
    own_buf[:, width:] = jnp.where(first, other[0:half], other[half:])
    copies = [pltpu.make_async_copy(full_buf, full_ref, sems.at[0]), pltpu.make_async_copy(own_buf, own_ref, sems.at[1])]
    for c in copies:
        c.start()
    owners = out_ref.shape[0] // capacity
    stride = slots // owners
    col = id_col(ids)
    parts = 2
    for k in range(parts):
        at = slice(k * slots // parts, (k + 1) * slots // parts)
        total = jnp.sum(jnp.where(col[at] == ids, dist, 0.0), axis=1, keepdims=True)
        scaled = new_ref[at, :] / (total / weight_ref[at, 0:1])
        few = owners // parts
        to = slice(k * few * capacity, (k + 1) * few * capacity)
        if stride == capacity:
            buf[to, :] = scaled.astype(BF16)
        for b in range(few if stride != capacity else 0):
            at = (k * few + b) * capacity
            buf[at : at + capacity, :] = scaled[b * stride : b * stride + capacity].astype(BF16)
        copies.append(pltpu.make_async_copy(buf.at[to, :], out_ref.at[to, :], sems.at[2 + k]))
        copies[-1].start()
    for c in copies:
        c.wait()


def join_kernel(*refs):
    pieces, joined = refs[:-1], refs[-1]
    at = 0
    for p in pieces:
        joined[at : at + p.shape[0], :] = p[...]
        at += p.shape[0]


def again_kernel(after_ref, value_ref, out_ref):
    out_ref[...] = value_ref[...]


def owner_kernel(ids_ref, dist_ref, got_ref, bank_ref, old_ref, new_ref, conc_ref):
    block = bank_ref.shape[0]
    slots = got_ref.shape[0]
    base = pl.program_id(0) * block
    same = jnp.where(iota((block, slots), 0) + base == ids_ref[...], 1.0, 0.0)
    width = bank_ref.shape[1]
    sums = nn(same.astype(BF16), got_ref[...])
    new_ref[...] = blend(bank_ref[...], sums[:, 0:width], sums[:, width : width + 1])
    turned = iota((slots, block), 1) + base == id_col(ids_ref[...])
    counts = jnp.sum(jnp.where(turned, 1.0, 0.0), axis=0, keepdims=True)
    total = jnp.sum(jnp.where(turned, to_col(dist_ref[...])[:, 0:1], 0.0), axis=0, keepdims=True)
    conc_ref[...] = jnp.where(counts > 0, total / weight_of(counts), old_ref[...])


def owner_call(ids, dist, got, bank, old):
    owned, width = bank.shape
    slots = got.shape[0]
    block = 256
    whole = lambda k: (0, 0)
    return pl.pallas_call(
        owner_kernel,
        grid=(owned // block,),
        in_specs=[
            pl.BlockSpec((1, slots), whole),
            pl.BlockSpec((1, slots), whole),
            pl.BlockSpec(got.shape, whole),
            pl.BlockSpec((block, width), lambda k: (k, 0)),
            pl.BlockSpec((1, block), lambda k: (0, k)),
        ],
        out_specs=[pl.BlockSpec((block, width), lambda k: (k, 0)), pl.BlockSpec((1, block), lambda k: (0, k))],
        out_shape=[shape((owned, width), F32), shape((1, owned), F32)],
        name="owner_kernel",
        compiler_params=pltpu.CompilerParams(vmem_limit_bytes=VMEM),
        cost_estimate=pl.CostEstimate(flops=20000000000, bytes_accessed=8 * owned * width, transcendentals=0),
    )(ids, dist, got, placed(bank, pltpu.HBM), placed(old, pltpu.HBM))


def logits_kernel(after_ref, mine_ref, other_ref, *refs):
    parts, (weight_ref, negs_ref, stats_ref) = refs[:-3], refs[-3:]
    rows, width = mine_ref.shape
    at = 0
    for p in parts:
        negs_ref[at : at + p.shape[0], :] = p[...]
        at += p.shape[0]
    logits = nt(mine_ref[...], negs_ref[:, 0:width]) + nt(other_ref[...], negs_ref[:, width:])
    top = jnp.max(logits, axis=1, keepdims=True)
    weight = jnp.exp(logits - top)
    weight_ref[...] = weight.astype(BF16)
    total = jnp.sum(weight, axis=1, keepdims=True)
    lane = iota((rows, LANES), 1)
    stats = jnp.transpose(jnp.where(lane == 0, top, jnp.where(lane == 1, total, 0.0)))
    stats_ref[...] = stats[0:8, :]


def pull_kernel(weight_ref, negs_ref, far_ref):
    far_ref[...] = nn(weight_ref[...], negs_ref[:, far_ref.shape[1] :])


def near_kernel(after_ref, weight_ref, negs_ref, near_ref):
    near_ref[...] = nn(weight_ref[...], negs_ref[:, 0 : near_ref.shape[1]])


def positive_kernel(slot_ref, query_ref, back_ref, rows_ref, part_ref):
    rows, slots = query_ref.shape[0], back_ref.shape[0]
    found = nn(onehot(iota((rows, slots), 1) == slot_ref[:, 0:1]), back_ref[...])
    rows_ref[...] = found.astype(BF16)
    part = to_row(jnp.sum(query_ref[...].astype(F32) * found, axis=1, keepdims=True))
    part_ref[...] = jnp.broadcast_to(part, part_ref.shape)


def factor_kernel(part_ref, far_ref, here_ref, there_ref, line_ref, factor_ref):
    rows = part_ref.shape[1]
    first = lax.axis_index("mp") == 0
    here, there = here_ref[0:2, :], there_ref[0:2, :]
    low = jnp.where(first, here, there)
    high = jnp.where(first, there, here)
    positive = part_ref[0:1, :] + far_ref[0:1, :]
    top = jnp.maximum(jnp.maximum(low[0:1], high[0:1]), positive)
    first_exp, last_exp, exppos = jnp.exp(low[0:1] - top), jnp.exp(high[0:1] - top), jnp.exp(positive - top)
    total = low[1:2] * first_exp + high[1:2] * last_exp + exppos
    once = 1.0 / total
    line_ref[...] = jnp.concatenate([total, top - positive], axis=0)
    mine, other = jnp.where(first, first_exp, last_exp) * once, jnp.where(first, last_exp, first_exp) * once
    factors = jnp.concatenate([mine, other, exppos * once - 1.0, jnp.zeros((LANES - 3, rows), F32)], axis=0)
    factor_ref[...] = jnp.transpose(factors)


def final_kernel(factor_ref, rows_ref, keep_ref, sent_ref, line_ref, grad_ref, loss_ref, grad_buf, loss_buf, sems):
    rows = keep_ref.shape[0]
    half = rows // 2
    copies = []
    for k in range(2):
        at = slice(k * half, (k + 1) * half)
        mine, other, pull = (factor_ref[at, j : j + 1] for j in range(3))
        grad_buf[at, :] = keep_ref[at, :] * mine + sent_ref[at, :] * other + pull * rows_ref[at, :].astype(F32)
        copies.append(pltpu.make_async_copy(grad_buf.at[at, :], grad_ref.at[at, :], sems.at[k]))
        copies[-1].start()
    loss_buf[...] = jnp.log(line_ref[0:1, :]) + line_ref[1:2, :]
    copies.append(pltpu.make_async_copy(loss_buf, loss_ref, sems.at[2]))
    copies[-1].start()
    for c in copies:
        c.wait()


def swap(value):
    return lax.ppermute(value, "mp", [(0, 1), (1, 0)])


def hop(value, count, bits):
    return lax.ppermute(value, "dp", [(k, k ^ bits) for k in range(count)])


def two_hop(value, count, bits):
    return lax.ppermute(
        value, ("dp", "mp"), [(2 * k + c, 2 * (k ^ bits[c]) + c) for k in range(count) for c in range(2)]
    )


def body(features, labels, queries, bank, old_conc, neg_index):
    count = lax.axis_size("dp")
    owned, width = bank.shape
    rows = features.shape[0]
    capacity = 3 * rows // count
    stride = 8 * -(-capacity // 8)
    block = stride * (width // LANES) + 8
    slots = count * stride
    negs = neg_index.shape[0] // count
    half = negs // 2
    loads = [pltpu.VMEM((1, rows), I32), pltpu.VMEM((rows, width), BF16)]

    label_row = labels.reshape(1, rows)
    (send,) = call(
        functools.partial(pack_kernel, count, owned, stride),
        (shape((count * block, LANES), BF16),),
        label_row, features, flops=2 * slots * rows * width, hbm=(0, 1), out_hbm=(0,),
        scratch=[*loads, pltpu.VMEM((count * block, LANES), BF16), pltpu.SemaphoreType.DMA((6,))],
    )
    query_far = swap(queries)
    got = exchange(send.reshape(count, block, LANES), OUT)
    got = got.reshape(count * block, LANES)

    neg_col, old_col, held, parts, spread = call(
        functools.partial(split_kernel, stride),
        (
            shape((negs, LANES), I32), shape((negs, LANES), F32), shape((negs, width), F32),
            shape((owned, 2 * width), BF16), shape((LANES, slots), BF16),
        ),
        neg_index.reshape(count, negs), old_conc.reshape(1, owned), bank, hbm=(2,), free=(0, 1),
        scratch=[pltpu.VMEM((owned, width), F32), pltpu.SemaphoreType.DMA],
    )
    extra = 8 * -(-slots // (8 * width))
    ids, new, pack, got, counts, neg_counts = call(
        functools.partial(mean_kernel, count),
        (
            shape((1, slots), I32), shape((slots, width), F32), shape((negs + extra, width), F32),
            shape((slots, width + LANES), BF16), shape((slots, LANES), F32), shape((negs, LANES), F32),
        ),
        query_far, neg_col, held, parts, spread, got, flops=8 * slots * owned * width, hbm=(0,),
        scratch=[pltpu.VMEM((2 * count, LANES), F32)],
    )
    weights, slot, query = call(
        functools.partial(prepare_kernel, count, owned, capacity),
        (shape((slots, LANES), F32), shape((rows, LANES), I32), shape((rows, width), BF16)),
        counts, label_row, queries, free=(1, 2),
    )
    full, own, dist, scaled, own_near = call(
        functools.partial(scale_kernel, capacity),
        (
            shape((negs, 2 * width), BF16), shape((half, 2 * width), BF16), shape((1, slots), F32),
            shape((count * capacity, width), BF16), shape((half, 2 * width), BF16),
        ),
        ids, neg_col, neg_counts, old_col, pack, new, weights, swap(pack), out_hbm=(0, 1, 3),
        scratch=[
            pltpu.VMEM((negs, 2 * width), BF16), pltpu.VMEM((count * capacity, width), BF16),
            pltpu.SemaphoreType.DMA((4,)),
        ],
    )
    step = count // 4
    line = [own_near, two_hop(full, count, (step, 2 * step)), hop(own, count, 3 * step)]
    (joined,) = call(join_kernel, (shape((sum(p.shape[0] for p in line), 2 * width), BF16),), *line)
    back = exchange(scaled.reshape(count, capacity, width), BACK)
    new_bank, new_conc = owner_call(ids, dist, got, bank, old_conc.reshape(1, owned))
    if step == 4:
        first = two_hop(joined, count, (1, 2))
        second = two_hop(joined, count, (2, 1))
        (again,) = call(again_kernel, (shape(joined.shape, BF16),), new_conc, first, hbm=(0,))
        pieces = [joined, again, second, two_hop(again, count, (2, 1))]
    while step > 1 and step != 4:
        few = min(4, step)
        step //= few
        pieces = [joined] + [hop(joined, count, step * k) for k in range(1, few)]
        if step > 1:
            joined = jnp.concatenate(pieces, axis=0)
    found, part = call(
        positive_kernel,
        (shape((rows, width), BF16), shape((8, rows), F32)),
        slot, query, back.reshape(count * capacity, width), flops=2 * slots * rows * width,
    )
    weight, all_negs, stats = call(
        logits_kernel,
        (shape((rows, half * count), BF16), shape((half * count, 2 * width), BF16), shape((8, rows), F32)),
        part, query, query_far, *pieces, flops=4 * rows * half * count * width, free=range(2, 99),
    )
    far_stats = swap(stats)
    flops = 2 * rows * half * count * width
    (sent,) = call(pull_kernel, (shape((rows, width), F32),), weight, all_negs, flops=flops)
    (keep,) = call(near_kernel, (shape((rows, width), F32),), sent, weight, all_negs, flops=flops)
    sent = swap(sent)
    line, factors = call(
        factor_kernel,
        (shape((2, rows), F32), shape((rows, LANES), F32)),
        part, swap(part), stats, far_stats,
    )
    grad, loss = call(
        final_kernel,
        (shape((rows, width), F32), shape((1, rows), F32)),
        factors, found, keep, sent, line, out_hbm=(0, 1),
        scratch=[pltpu.VMEM((rows, width), F32), pltpu.VMEM((1, rows), F32), pltpu.SemaphoreType.DMA((3,))],
    )
    return (new_bank, new_conc.reshape(owned), loss.reshape(rows), grad)


def solution(mesh):
    placed = (P("dp", "mp"), P("dp"), P("dp", "mp"), P("dp", "mp"), P("dp"), P())
    return jax.shard_map(
        body,
        mesh=mesh,
        in_specs=placed,
        out_specs=(P("dp", "mp"), P("dp"), P("dp"), P("dp", "mp")),
        check_vma=False,
    )
```

```python
import functools

import jax
import jax.numpy as jnp
from jax import lax
from jax.experimental import pallas as pl
from jax.experimental.pallas import tpu as pltpu
from jax.sharding import PartitionSpec as P

F32 = jnp.float32
BF16 = jnp.bfloat16
I32 = jnp.int32
LANES = 128
VMEM = 24 * 2**20
OUT = (7, 14, 5, 13, 1, 10, 15, 11, 0, 2, 3, 9, 8, 12, 6, 4)
BACK = (4, 0, 5, 6, 8, 12, 2, 3, 1, 11, 9, 13, 15, 10, 14, 7)


def call(kernel, outs, *args, flops=0, hbm=(), out_hbm=(), free=(), out_free=(), scratch=()):
    moved = sum(a.size * a.dtype.itemsize for a in args) + sum(o.size * o.dtype.itemsize for o in outs)
    spaces = [pltpu.HBM if k in hbm else pltpu.VMEM for k in range(len(args))]
    out_spaces = [pltpu.HBM if k in out_hbm else pltpu.VMEM for k in range(len(outs))]
    return pl.pallas_call(
        kernel,
        out_shape=[o if k in out_free else space(o.shape, o.dtype) for k, (o, space) in enumerate(zip(outs, out_spaces))],
        in_specs=[pl.BlockSpec(memory_space=space) for space in spaces],
        out_specs=[pl.BlockSpec(memory_space=space) for space in out_spaces],
        scratch_shapes=list(scratch),
        name=getattr(kernel, "func", kernel).__name__,
        compiler_params=pltpu.CompilerParams(vmem_limit_bytes=VMEM),
        cost_estimate=pl.CostEstimate(flops=flops, bytes_accessed=moved, transcendentals=0),
    )(*[placed(a, space, k in free) for k, (a, space) in enumerate(zip(args, spaces))])


def placed(value, space, free=False):
    return value if free else pltpu.with_memory_space_constraint(value, space)


def shape(dims, dtype):
    return jax.ShapeDtypeStruct(dims, dtype)


def nt(a, b):
    return lax.dot_general(a, b, (((1,), (1,)), ((), ())), preferred_element_type=F32)


def nn(a, b):
    return jnp.dot(a, b, preferred_element_type=F32)


def iota(dims, axis):
    return lax.broadcasted_iota(I32, dims, axis)


def onehot(mask):
    return jnp.where(mask, 1.0, 0.0).astype(BF16)


def to_col(row):
    return jnp.transpose(jnp.broadcast_to(row, (LANES, row.shape[1])))


def to_row(col):
    return jnp.transpose(jnp.broadcast_to(col, (col.shape[0], LANES)))[0:1, :]


def id_col(ids):
    return to_col(ids.astype(F32))[:, 0:1].astype(I32)


def ahead(rows):
    return onehot(iota((rows, rows), 0) <= iota((rows, rows), 1))


def ranks_of(label, owners, owned, before):
    start = iota((owners, label.shape[1]), 0) * owned
    mine = (label >= start) & (label < start + owned)
    running = nn(onehot(mine), before)
    return mine, jnp.sum(jnp.where(mine, running, 0.0), axis=0, keepdims=True) - 1.0


def order_of(owners, order):
    return order if owners == len(order) else tuple(range(owners))


def slot_of(mine, rank, stride, order):
    owners = mine.shape[0]
    owner = place = iota(mine.shape, 0)
    for k, device in enumerate(order_of(owners, order)):
        place = jnp.where(owner == device, k, place) if k != device else place
    place = jnp.sum(jnp.where(mine, place.astype(F32), 0.0), axis=0, keepdims=True)
    return (place * stride + rank).astype(I32)


def exchange(value, order):
    groups = [list(order_of(lax.axis_size("dp"), order))]
    return lax.all_to_all(value, "dp", split_axis=0, concat_axis=0, axis_index_groups=groups)


def pack_kernel(owners, owned, stride, label_ref, feat_ref, send_ref, label_buf, feat_buf, send_buf, sems):
    rows, width = feat_buf.shape
    block = send_buf.shape[0] // owners
    labels = pltpu.make_async_copy(label_ref, label_buf, sems.at[0])
    feats = pltpu.make_async_copy(feat_ref, feat_buf, sems.at[1])
    labels.start()
    feats.start()
    before = ahead(rows)
    labels.wait()
    label = label_buf[...]
    mine, rank = ranks_of(label, owners, owned, before)
    slot = slot_of(mine, rank, stride, OUT)
    value = jnp.where(mine, (label - iota((owners, rows), 0) * owned + 1).astype(F32), 0.0)
    high = jnp.floor(value * (1.0 / 32.0))
    value = jnp.concatenate([high, value - 32.0 * high], axis=0).astype(BF16)
    ids = nt(value, onehot(iota((LANES, rows), 0).astype(F32) == rank))
    feats.wait()
    chunks = 4
    part = owners // chunks
    copies = []
    row = iota((8, LANES), 0)
    for k in range(chunks):
        spot = iota((part * stride, rows), 0) + k * part * stride
        picked = nn(onehot(spot == slot), feat_buf[...]).astype(BF16)
        for c in range(part):
            b = k * part + c
            for j in range(width // LANES):
                piece = picked[c * stride : (c + 1) * stride, j * LANES : (j + 1) * LANES]
                send_buf[b * block + j * stride : b * block + (j + 1) * stride, :] = piece
            o = order_of(owners, OUT)[b]
            tail = jnp.where(row == 0, ids[o : o + 1], jnp.where(row == 1, ids[owners + o : owners + o + 1], 0.0))
            send_buf[(b + 1) * block - 8 : (b + 1) * block, :] = tail.astype(BF16)
        at = slice(k * part * block, (k + 1) * part * block)
        copies.append(pltpu.make_async_copy(send_buf.at[at, :], send_ref.at[at, :], sems.at[2 + k]))
        copies[k].start()
    for c in copies:
        c.wait()


def split_kernel(keep, neg_ref, old_ref, bank_ref, neg_col_ref, old_col_ref, held_ref, parts_ref, spread_ref, bank_buf, sem):
    owned, width = bank_buf.shape
    negs = neg_ref.shape[1]
    load = pltpu.make_async_copy(bank_ref, bank_buf, sem)
    load.start()
    me = lax.axis_index("dp").astype(I32)
    wanted = neg_ref[pl.ds(me, 1), :] - me * owned
    wanted = jnp.concatenate([wanted] * (LANES // negs), axis=1)
    neg_col = id_col(wanted)[0:negs, :]
    neg_col_ref[...] = jnp.broadcast_to(neg_col, neg_col_ref.shape)
    same = neg_col == iota((negs, owned), 1)
    old = jnp.sum(jnp.where(same, old_ref[...], 0.0), axis=1, keepdims=True)
    old_col_ref[...] = jnp.broadcast_to(old, old_col_ref.shape)
    pick = onehot(same)
    place = iota(spread_ref.shape, 1).astype(F32)
    within = place - keep * jnp.floor((place + 0.5) * (1.0 / keep))
    spread_ref[...] = onehot(within == iota(spread_ref.shape, 0).astype(F32))
    load.wait()
    bank = bank_buf[...]
    high = bank.astype(BF16)
    rest = bank - high.astype(F32)
    middle = rest.astype(BF16)
    low = (rest - middle.astype(F32)).astype(BF16)
    parts_ref[:, 0:width] = high
    parts_ref[:, width : 2 * width] = middle
    held_ref[...] = nn(pick, high) + nn(pick, middle) + nn(pick, low)


def blend(bank, sums, counts):
    safe = jnp.maximum(counts, 1.0)
    return jnp.where(counts > 0, 0.5 * bank + 0.5 * sums / safe, bank)


def mean_kernel(
    owners, after_ref, neg_ref, held_ref, parts_ref, spread_ref, got_ref,
    ids_ref, new_ref, pack_ref, rows_ref, count_ref, neg_count_ref, table,
):
    owned = parts_ref.shape[0]
    negs, width = held_ref.shape
    slots = new_ref.shape[0]
    keep = slots // owners
    block = got_ref.shape[0] // owners
    for b in range(owners):
        c = order_of(owners, OUT).index(order_of(owners, BACK)[b])
        sent = got_ref[(c + 1) * block - 8 : (c + 1) * block, :].astype(F32)
        table[b : b + 1, :] = sent[0:1]
        table[owners + b : owners + b + 1, :] = sent[1:2]
        for j in range(width // LANES):
            at = c * block + j * keep
            rows_ref[b * keep : (b + 1) * keep, j * LANES : (j + 1) * LANES] = got_ref[at : at + keep, :]
    rows_ref[:, width:] = jnp.ones((slots, LANES), BF16)
    wide = nn(table[...].astype(BF16), spread_ref[...])
    wide = 32.0 * wide[0:owners] + wide[owners:]
    first = iota((owners, slots), 0) * keep
    spot = iota((owners, slots), 1)
    ids = jnp.sum(jnp.where((spot >= first) & (spot < first + keep), wide, 0.0), axis=0, keepdims=True)
    ids = jnp.where(ids > 0.5, ids - 1.0, float(owned)).astype(I32)
    ids_ref[...] = ids
    got = rows_ref[...]
    col = id_col(ids)
    block = 256 if slots % 256 == 0 else slots
    sums = nn(onehot(neg_ref[:, 0:1] == ids), got)
    neg_count_ref[...] = sums[:, width:]
    pack_ref[0:negs, :] = blend(held_ref[...], sums[:, 0:width], sums[:, width : width + 1])
    squares = []
    for k in range(slots // block):
        at = slice(k * block, (k + 1) * block)
        picked = nn(onehot(iota((block, owned), 1) == col[at]), parts_ref[...])
        sums = nn(onehot(col[at] == ids), got)
        count_ref[at, :] = sums[:, width:]
        new = blend(picked[:, 0:width] + picked[:, width:], sums[:, 0:width], sums[:, width : width + 1])
        new_ref[at, :] = new
        differ = got[at, 0:width].astype(F32) - new
        squares.append(to_row(jnp.sum(differ * differ, axis=1, keepdims=True)))
    squared = jnp.concatenate(squares, axis=1)
    for k in range(-(-slots // width)):
        piece = squared[:, k * width : min((k + 1) * width, slots)]
        pack_ref[negs + k : negs + k + 1, 0 : piece.shape[1]] = piece


def weight_of(counts):
    safe = jnp.maximum(counts, 1.0)
    return safe * jnp.log(safe + 10.0)


def prepare_kernel(owners, owned, capacity, count_ref, label_ref, query_ref, weight_ref, slot_ref, copy_ref):
    weight_ref[...] = weight_of(count_ref[...])
    slot = slot_of(*ranks_of(label_ref[...], owners, owned, ahead(label_ref.shape[1])), capacity, BACK)
    slot_ref[...] = to_col(slot.astype(F32)).astype(I32)
    copy_ref[...] = query_ref[...]


def scale_kernel(
    capacity, ids_ref, neg_ref, count_ref, old_ref, pack_ref, new_ref, weight_ref, other_ref,
    full_ref, own_ref, dist_ref, out_ref, own_buf, full_buf, buf, sems,
):
    slots, width = new_ref.shape
    negs = neg_ref.shape[0]
    half = negs // 2
    ids = ids_ref[...]
    pieces = []
    for k in range(-(-slots // width)):
        part = pack_ref[negs + k : negs + k + 1, :] + other_ref[negs + k : negs + k + 1, :]
        pieces.append(part[:, 0 : min(width, slots - k * width)])
    dist = jnp.sqrt(jnp.concatenate(pieces, axis=1) + 0.25)
    dist_ref[...] = dist
    total = jnp.sum(jnp.where(neg_ref[:, 0:1] == ids, dist, 0.0), axis=1, keepdims=True)
    counts = count_ref[:, 0:1]
    conc = jnp.where(counts > 0, total / weight_of(counts), old_ref[:, 0:1])
    mine = (pack_ref[0:negs, :] / conc).astype(BF16)
    other = (other_ref[0:negs, :] / conc).astype(BF16)
    full_buf[:, 0:width] = mine
    full_buf[:, width:] = other
    first = lax.axis_index("mp") == 0
    own_buf[:, 0:width] = jnp.where(first, mine[0:half], mine[half:])
    own_buf[:, width:] = jnp.where(first, other[0:half], other[half:])
    copies = [pltpu.make_async_copy(full_buf, full_ref, sems.at[0]), pltpu.make_async_copy(own_buf, own_ref, sems.at[1])]
    for c in copies:
        c.start()
    owners = out_ref.shape[0] // capacity
    stride = slots // owners
    col = id_col(ids)
    parts = 2
    for k in range(parts):
        at = slice(k * slots // parts, (k + 1) * slots // parts)
        total = jnp.sum(jnp.where(col[at] == ids, dist, 0.0), axis=1, keepdims=True)
        scaled = new_ref[at, :] / (total / weight_ref[at, 0:1])
        few = owners // parts
        to = slice(k * few * capacity, (k + 1) * few * capacity)
        if stride == capacity:
            buf[to, :] = scaled.astype(BF16)
        for b in range(few if stride != capacity else 0):
            at = (k * few + b) * capacity
            buf[at : at + capacity, :] = scaled[b * stride : b * stride + capacity].astype(BF16)
        copies.append(pltpu.make_async_copy(buf.at[to, :], out_ref.at[to, :], sems.at[2 + k]))
        copies[-1].start()
    for c in copies:
        c.wait()


def join_kernel(*refs):
    pieces, joined = refs[:-1], refs[-1]
    at = 0
    for p in pieces:
        joined[at : at + p.shape[0], :] = p[...]
        at += p.shape[0]


def again_kernel(after_ref, value_ref, out_ref):
    out_ref[...] = value_ref[...]


def owner_kernel(ids_ref, dist_ref, got_ref, bank_ref, old_ref, new_ref, conc_ref):
    block = bank_ref.shape[0]
    slots = got_ref.shape[0]
    base = pl.program_id(0) * block
    same = jnp.where(iota((block, slots), 0) + base == ids_ref[...], 1.0, 0.0)
    width = bank_ref.shape[1]
    sums = nn(same.astype(BF16), got_ref[...])
    new_ref[...] = blend(bank_ref[...], sums[:, 0:width], sums[:, width : width + 1])
    turned = iota((slots, block), 1) + base == id_col(ids_ref[...])
    counts = jnp.sum(jnp.where(turned, 1.0, 0.0), axis=0, keepdims=True)
    total = jnp.sum(jnp.where(turned, to_col(dist_ref[...])[:, 0:1], 0.0), axis=0, keepdims=True)
    conc_ref[...] = jnp.where(counts > 0, total / weight_of(counts), old_ref[...])


def owner_call(ids, dist, got, bank, old):
    owned, width = bank.shape
    slots = got.shape[0]
    block = 256
    whole = lambda k: (0, 0)
    return pl.pallas_call(
        owner_kernel,
        grid=(owned // block,),
        in_specs=[
            pl.BlockSpec((1, slots), whole),
            pl.BlockSpec((1, slots), whole),
            pl.BlockSpec(got.shape, whole),
            pl.BlockSpec((block, width), lambda k: (k, 0)),
            pl.BlockSpec((1, block), lambda k: (0, k)),
        ],
        out_specs=[pl.BlockSpec((block, width), lambda k: (k, 0)), pl.BlockSpec((1, block), lambda k: (0, k))],
        out_shape=[shape((owned, width), F32), shape((1, owned), F32)],
        name="owner_kernel",
        compiler_params=pltpu.CompilerParams(vmem_limit_bytes=VMEM),
        cost_estimate=pl.CostEstimate(flops=20000000000, bytes_accessed=8 * owned * width, transcendentals=0),
    )(ids, dist, got, placed(bank, pltpu.HBM), placed(old, pltpu.HBM))


def logits_kernel(after_ref, mine_ref, other_ref, *refs):
    parts, (weight_ref, negs_ref, stats_ref) = refs[:-3], refs[-3:]
    rows, width = mine_ref.shape
    at = 0
    for p in parts:
        negs_ref[at : at + p.shape[0], :] = p[...]
        at += p.shape[0]
    logits = nt(mine_ref[...], negs_ref[:, 0:width]) + nt(other_ref[...], negs_ref[:, width:])
    top = jnp.max(logits, axis=1, keepdims=True)
    weight = jnp.exp(logits - top)
    weight_ref[...] = weight.astype(BF16)
    total = jnp.sum(weight, axis=1, keepdims=True)
    lane = iota((rows, LANES), 1)
    stats = jnp.transpose(jnp.where(lane == 0, top, jnp.where(lane == 1, total, 0.0)))
    stats_ref[...] = stats[0:8, :]


def pull_kernel(weight_ref, negs_ref, far_ref):
    far_ref[...] = nn(weight_ref[...], negs_ref[:, far_ref.shape[1] :])


def near_kernel(after_ref, weight_ref, negs_ref, near_ref):
    near_ref[...] = nn(weight_ref[...], negs_ref[:, 0 : near_ref.shape[1]])


def positive_kernel(slot_ref, query_ref, back_ref, rows_ref, part_ref):
    rows, slots = query_ref.shape[0], back_ref.shape[0]
    found = nn(onehot(iota((rows, slots), 1) == slot_ref[:, 0:1]), back_ref[...])
    rows_ref[...] = found.astype(BF16)
    part = to_row(jnp.sum(query_ref[...].astype(F32) * found, axis=1, keepdims=True))
    part_ref[...] = jnp.broadcast_to(part, part_ref.shape)


def factor_kernel(part_ref, far_ref, here_ref, there_ref, line_ref, factor_ref):
    rows = part_ref.shape[1]
    first = lax.axis_index("mp") == 0
    here, there = here_ref[0:2, :], there_ref[0:2, :]
    low = jnp.where(first, here, there)
    high = jnp.where(first, there, here)
    positive = part_ref[0:1, :] + far_ref[0:1, :]
    top = jnp.maximum(jnp.maximum(low[0:1], high[0:1]), positive)
    first_exp, last_exp, exppos = jnp.exp(low[0:1] - top), jnp.exp(high[0:1] - top), jnp.exp(positive - top)
    total = low[1:2] * first_exp + high[1:2] * last_exp + exppos
    once = 1.0 / total
    line_ref[...] = jnp.concatenate([total, top - positive], axis=0)
    mine, other = jnp.where(first, first_exp, last_exp) * once, jnp.where(first, last_exp, first_exp) * once
    factors = jnp.concatenate([mine, other, exppos * once - 1.0, jnp.zeros((LANES - 3, rows), F32)], axis=0)
    factor_ref[...] = jnp.transpose(factors)


def final_kernel(factor_ref, rows_ref, keep_ref, sent_ref, line_ref, grad_ref, loss_ref, grad_buf, loss_buf, sems):
    rows = keep_ref.shape[0]
    half = rows // 2
    copies = []
    for k in range(2):
        at = slice(k * half, (k + 1) * half)
        mine, other, pull = (factor_ref[at, j : j + 1] for j in range(3))
        grad_buf[at, :] = keep_ref[at, :] * mine + sent_ref[at, :] * other + pull * rows_ref[at, :].astype(F32)
        copies.append(pltpu.make_async_copy(grad_buf.at[at, :], grad_ref.at[at, :], sems.at[k]))
        copies[-1].start()
    loss_buf[...] = jnp.log(line_ref[0:1, :]) + line_ref[1:2, :]
    copies.append(pltpu.make_async_copy(loss_buf, loss_ref, sems.at[2]))
    copies[-1].start()
    for c in copies:
        c.wait()


def swap(value):
    return lax.ppermute(value, "mp", [(0, 1), (1, 0)])


def hop(value, count, bits):
    return lax.ppermute(value, "dp", [(k, k ^ bits) for k in range(count)])


def two_hop(value, count, bits):
    return lax.ppermute(
        value, ("dp", "mp"), [(2 * k + c, 2 * (k ^ bits[c]) + c) for k in range(count) for c in range(2)]
    )


def body(features, labels, queries, bank, old_conc, neg_index):
    count = lax.axis_size("dp")
    owned, width = bank.shape
    rows = features.shape[0]
    capacity = 3 * rows // count
    stride = 8 * -(-capacity // 8)
    block = stride * (width // LANES) + 8
    slots = count * stride
    negs = neg_index.shape[0] // count
    half = negs // 2
    loads = [pltpu.VMEM((1, rows), I32), pltpu.VMEM((rows, width), BF16)]

    label_row = labels.reshape(1, rows)
    (send,) = call(
        functools.partial(pack_kernel, count, owned, stride),
        (shape((count * block, LANES), BF16),),
        label_row, features, flops=2 * slots * rows * width, hbm=(0, 1), out_hbm=(0,),
        scratch=[*loads, pltpu.VMEM((count * block, LANES), BF16), pltpu.SemaphoreType.DMA((6,))],
    )
    query_far = swap(queries)
    got = exchange(send.reshape(count, block, LANES), OUT)
    got = got.reshape(count * block, LANES)

    neg_col, old_col, held, parts, spread = call(
        functools.partial(split_kernel, stride),
        (
            shape((negs, LANES), I32), shape((negs, LANES), F32), shape((negs, width), F32),
            shape((owned, 2 * width), BF16), shape((LANES, slots), BF16),
        ),
        neg_index.reshape(count, negs), old_conc.reshape(1, owned), bank, hbm=(2,), free=(0, 1),
        scratch=[pltpu.VMEM((owned, width), F32), pltpu.SemaphoreType.DMA],
    )
    extra = 8 * -(-slots // (8 * width))
    ids, new, pack, got, counts, neg_counts = call(
        functools.partial(mean_kernel, count),
        (
            shape((1, slots), I32), shape((slots, width), F32), shape((negs + extra, width), F32),
            shape((slots, width + LANES), BF16), shape((slots, LANES), F32), shape((negs, LANES), F32),
        ),
        query_far, neg_col, held, parts, spread, got, flops=8 * slots * owned * width, hbm=(0,),
        scratch=[pltpu.VMEM((2 * count, LANES), F32)],
    )
    weights, slot, query = call(
        functools.partial(prepare_kernel, count, owned, capacity),
        (shape((slots, LANES), F32), shape((rows, LANES), I32), shape((rows, width), BF16)),
        counts, label_row, queries, free=(1, 2),
    )
    full, own, dist, scaled, own_near = call(
        functools.partial(scale_kernel, capacity),
        (
            shape((negs, 2 * width), BF16), shape((half, 2 * width), BF16), shape((1, slots), F32),
            shape((count * capacity, width), BF16), shape((half, 2 * width), BF16),
        ),
        ids, neg_col, neg_counts, old_col, pack, new, weights, swap(pack), out_hbm=(0, 1, 3),
        scratch=[
            pltpu.VMEM((negs, 2 * width), BF16), pltpu.VMEM((count * capacity, width), BF16),
            pltpu.SemaphoreType.DMA((4,)),
        ],
    )
    step = count // 4
    line = [own_near, two_hop(full, count, (step, 2 * step)), hop(own, count, 3 * step)]
    (joined,) = call(join_kernel, (shape((sum(p.shape[0] for p in line), 2 * width), BF16),), *line)
    back = exchange(scaled.reshape(count, capacity, width), BACK)
    new_bank, new_conc = owner_call(ids, dist, got, bank, old_conc.reshape(1, owned))
    if step == 4:
        first = two_hop(joined, count, (1, 2))
        second = two_hop(joined, count, (2, 1))
        (again,) = call(again_kernel, (shape(joined.shape, BF16),), new_conc, first, hbm=(0,))
        pieces = [joined, again, second, two_hop(again, count, (2, 1))]
    while step > 1 and step != 4:
        few = min(4, step)
        step //= few
        pieces = [joined] + [hop(joined, count, step * k) for k in range(1, few)]
        if step > 1:
            joined = jnp.concatenate(pieces, axis=0)
    found, part = call(
        positive_kernel,
        (shape((rows, width), BF16), shape((8, rows), F32)),
        slot, query, back.reshape(count * capacity, width), flops=2 * slots * rows * width,
    )
    weight, all_negs, stats = call(
        logits_kernel,
        (shape((rows, half * count), BF16), shape((half * count, 2 * width), BF16), shape((8, rows), F32)),
        part, query, query_far, *pieces, flops=4 * rows * half * count * width, free=range(2, 99),
    )
    far_stats = swap(stats)
    flops = 2 * rows * half * count * width
    (sent,) = call(pull_kernel, (shape((rows, width), F32),), weight, all_negs, flops=flops)
    (keep,) = call(near_kernel, (shape((rows, width), F32),), sent, weight, all_negs, flops=flops)
    sent = swap(sent)
    line, factors = call(
        factor_kernel,
        (shape((2, rows), F32), shape((rows, LANES), F32)),
        part, swap(part), stats, far_stats,
    )
    grad, loss = call(
        final_kernel,
        (shape((rows, width), F32), shape((1, rows), F32)),
        factors, found, keep, sent, line, out_hbm=(0, 1),
        scratch=[pltpu.VMEM((rows, width), F32), pltpu.VMEM((1, rows), F32), pltpu.SemaphoreType.DMA((3,))],
    )
    return (new_bank, new_conc.reshape(owned), loss.reshape(rows), grad)


def solution(mesh):
    placed = (P("dp", "mp"), P("dp"), P("dp", "mp"), P("dp", "mp"), P("dp"), P())
    return jax.shard_map(
        body,
        mesh=mesh,
        in_specs=placed,
        out_specs=(P("dp", "mp"), P("dp"), P("dp"), P("dp", "mp")),
        check_vma=False,
    )
```
